128 devices in a mesh: chain: 32 (over x_hi, z, y), tm: 4 (over x_lo, core).
Axes of the slice: x: 4 (x_hi: 2, x_lo: 2; x = x_hi * 2 + x_lo), y: 4, z: 4, core: 2. Of those that a mesh axis runs over, the one named last changes fastest.
Arguments:
- traces: bfloat16 [2048, 128, 512], P('chain', 'tm'), may hold values from -6 to 6
Outputs:
- stack: float32 [2048, 2, 256, 256], P('chain', None, 'tm')
The draws below stay inside these ranges and needn't reach their ends.
All inputs are finite; a program needn't handle non-finite values.
Results may differ from the reference program's by a relative error of at most 0.012.
Values may be sent and summed in bfloat16 or wider, within the bound.
A program may use at most 256 MiB of HBM per device.

```python
import math
import jax
import jax.numpy as jnp
from jax import lax

CH_DEV = 64
LAG = 256
BINS = 256
WIN_DEV = 32
NSAMP = 512
SEGMENTS = 4
WINDOWS = 128
CHANNELS = 2048


def level_of(rng, shape, cuts, least, largest):
    level = 1.0
    for position, parts in cuts:
        heights = jax.random.uniform(jax.random.fold_in(jax.random.fold_in(rng, 6), position), (parts,), jnp.float32, least / len(cuts), largest / len(cuts))
        level = level * jnp.repeat(jnp.exp(heights), shape[position] // parts).reshape((-1,) + (1,) * (len(shape) - 1 - position))
    return level


def bell_draw(stream_key, extent, width, limit, split=(), kind=jnp.bfloat16):
    result = jax.random.normal(stream_key, extent, jnp.float32) * width
    if len(split) > 0:
        result = level_of(stream_key, extent, split, -0.22, 0.18) * result
    return jnp.clip(result, min=-limit, max=limit).astype(kind)


def setup_inputs(seed: int = 0) -> dict:
    key_list = jax.random.split(jax.random.key(seed), 2)
    return {
        "traces": bell_draw(key_list[0], (CHANNELS, WINDOWS, NSAMP), 1.0, 6.0, ((0, 32), (1, 4))),
    }


def kernel_table(length, bins):
    samples = jnp.arange(length, dtype=jnp.int32)
    freqs = jnp.arange(bins, dtype=jnp.int32)
    phase_index = samples[:, None] * freqs[None, :] % length
    angles = 2.0 * math.pi / length * phase_index.astype(jnp.float32)
    window_taper = 0.5 - 0.5 * jnp.cos(2.0 * math.pi / length * samples.astype(jnp.float32))
    cosines = window_taper[:, None] * jnp.cos(angles)
    sines = -window_taper[:, None] * jnp.sin(angles)
    return jnp.concatenate([cosines, sines], axis=1).astype(jnp.bfloat16)

def whiten(traces_block, kernel):
    channels, windows, length = traces_block.shape
    bins = kernel.shape[1] // 2
    spectra = jnp.dot(traces_block.reshape(channels * windows, length), kernel, preferred_element_type=jnp.float32)
    spectra = spectra.reshape(channels, windows, 2, bins)
    magnitude = jnp.sqrt(spectra[:, :, 0] * spectra[:, :, 0] + spectra[:, :, 1] * spectra[:, :, 1])
    mean_level = lax.optimization_barrier(jnp.mean(magnitude, axis=-1, keepdims=True))
    divisor = magnitude + 0.1 * (mean_level + 1e-06)
    return (spectra / divisor[:, :, None, :]).astype(jnp.bfloat16)

def lag_band(matrix, lags):
    leading = matrix.shape[:-2]
    channels = matrix.shape[-2]
    columns = matrix.shape[-1]
    flattened = matrix.reshape(leading + (channels * columns,))
    pad_spec = [(0, 0)] * len(leading) + [(0, channels)]
    flattened = jnp.pad(flattened, pad_spec)
    return flattened.reshape(leading + (channels, columns + 1))[..., :lags]

def segment_stack(own, reach, lags, scale):
    own_real = own[:, :, 0].astype(jnp.float32)
    own_imag = own[:, :, 1].astype(jnp.float32)
    left_rows = jnp.concatenate([jnp.concatenate([own_real, own_imag], axis=1), jnp.concatenate([own_imag, -own_real], axis=1)], axis=0)
    right_rows = jnp.concatenate([reach[:, :, 0], reach[:, :, 1]], axis=1).astype(jnp.float32)
    products = jnp.einsum('awf,jwf->faj', left_rows, right_rows)
    channels = own.shape[0]
    real_band = lag_band(products[:, :channels], lags)
    imag_band = lag_band(products[:, channels:], lags)
    stacked = jnp.stack([real_band, imag_band], axis=0)
    return (jnp.transpose(stacked, (2, 0, 1, 3)) * scale).astype(jnp.bfloat16)

def reference(traces):
    kernel = kernel_table(NSAMP, BINS)
    blocks = traces.reshape(CHANNELS // CH_DEV, CH_DEV, WINDOWS, NSAMP)

    def whiten_block(block):
        return whiten(block, kernel)
    whitened = lax.map(whiten_block, blocks).reshape(CHANNELS, WINDOWS, 2, BINS)
    padded = jnp.concatenate([whitened, jnp.zeros((LAG, WINDOWS, 2, BINS), jnp.bfloat16)], axis=0)
    scale = 1.0 / math.sqrt(WINDOWS)

    def one_block(index):
        first = (index * CH_DEV).astype(jnp.int32)
        own = lax.dynamic_slice_in_dim(whitened, first, CH_DEV, 0)
        reach = lax.dynamic_slice_in_dim(padded, first, CH_DEV + LAG, 0)
        total = jnp.zeros((CH_DEV, 2, BINS, LAG), jnp.float32)
        for segment in range(SEGMENTS):
            lower = segment * WIN_DEV
            upper = lower + WIN_DEV
            hour = segment_stack(own[:, lower:upper], reach[:, lower:upper], LAG, scale)
            total = total + lax.optimization_barrier(hour).astype(jnp.float32)
        return total
    stacks = lax.map(one_block, jnp.arange(CHANNELS // CH_DEV, dtype=jnp.int32))
    return stacks.reshape(CHANNELS, 2, BINS, LAG)
```

```python
import math

import jax
import jax.numpy as jnp
import numpy as np
from jax import lax
from jax.experimental import pallas as pl
from jax.experimental.pallas import tpu as pltpu
from jax.sharding import PartitionSpec as P

MESH = pl.DeviceIdType.MESH

CH = 64
LAG = 256
BINS = 256
WIN = 32
NSAMP = 512
SEG = 4
BAND = BINS // SEG
FCH = 8
NCH = BAND // FCH
NBLK = LAG // CH + 1
ROWY = 4
SCALE = 1.0 / math.sqrt(WIN * SEG)


def kernel_rows():
    samples = np.arange(NSAMP, dtype=np.int32)
    freqs = np.arange(BINS, dtype=np.int32)
    phase = (samples[:, None] * freqs[None, :]) % NSAMP
    angles = np.float32(2.0 * math.pi / NSAMP) * phase.astype(np.float32)
    taper = np.float32(0.5) - np.float32(0.5) * np.cos(
        np.float32(2.0 * math.pi / NSAMP) * samples.astype(np.float32)
    )
    cosines = taper[:, None] * np.cos(angles)
    sines = -taper[:, None] * np.sin(angles)
    table = np.stack([cosines.T, sines.T], axis=0).astype(np.float32)
    table = table.reshape(2, SEG, NCH, FCH, NSAMP).transpose(1, 2, 0, 3, 4)
    return table.reshape(2 * BINS, NSAMP).astype(jnp.bfloat16)


def stack_kernel(tr_ref, kt_ref, out_ref, wt, rx, ball, relay, prod, obuf,
                 a2a_send, a2a_recv, own_sem, blk_send, blk_recv, out_sem):
    chain = lax.axis_index("chain")
    me = lax.axis_index("tm")
    n_chain = lax.axis_size("chain")
    y = lax.rem(chain, ROWY)

    def peer(delta):
        return lax.rem(me + delta, SEG)

    first = y == 0
    last = y == ROWY - 1
    src1 = jnp.where(last, chain - (ROWY - 1), chain + 1)
    src3 = jnp.where(first, chain + (ROWY - 1), chain - 1)
    dst1 = jnp.where(first, chain + (ROWY - 1), chain - 1)
    dst3 = jnp.where(last, chain - (ROWY - 1), chain + 1)
    has4 = chain + ROWY < n_chain
    to4 = chain >= ROWY
    has2 = chain + 1 < n_chain
    to2 = chain >= 1

    barrier = pltpu.get_barrier_semaphore()

    def greet(c, t):
        pl.semaphore_signal(barrier, inc=1, device_id=(c, t), device_id_type=MESH)

    for delta in (1, 2, 3):
        greet(chain, peer(delta))
    greet(src1, me)
    greet(src3, me)
    pl.when(has4)(lambda: greet(chain + ROWY, me))
    pl.when(has2)(lambda: greet(chain + 1, me))

    cols = 256
    chans = cols // WIN

    def whiten(j, carry):
        tr = tr_ref[pl.ds(chans * j, chans)].reshape(cols, NSAMP)
        spec = lax.dot_general(kt_ref[...], tr, (((1,), (1,)), ((), ())),
                               preferred_element_type=jnp.float32)
        spec = spec.reshape(SEG * NCH, 2, FCH, cols)
        re = spec[:, 0]
        im = spec[:, 1]
        mag = jnp.sqrt(re * re + im * im)
        level = jnp.sum(mag, axis=(0, 1), keepdims=True) * (1.0 / BINS)
        inv = 1.0 / (mag + 0.1 * (level + 1e-6))
        white = jnp.stack([re * inv, im * inv], axis=1)
        white = white.reshape(SEG, NCH, 2 * FCH, cols).astype(jnp.bfloat16)
        wt[:, :, :, pl.ds(pl.multiple_of(cols * j, cols), cols)] = white
        return carry

    lax.fori_loop(0, CH // chans, whiten, 0)

    n_wait = 5 + to4.astype(jnp.int32) + to2.astype(jnp.int32)
    pl.semaphore_wait(barrier, n_wait)

    def a2a_copy(delta, k):
        return pltpu.make_async_remote_copy(
            src_ref=wt.at[peer(delta), k], dst_ref=rx.at[me, k],
            send_sem=a2a_send.at[delta - 1, k], recv_sem=a2a_recv.at[delta - 1, k],
            device_id=(chain, peer(delta)), device_id_type=MESH)

    def own_copy():
        return pltpu.make_async_copy(wt.at[me], rx.at[me], own_sem)

    own_copy().start()

    def start_a2a(k, carry):
        for delta in (1, 2, 3):
            a2a_copy(delta, k).start()
        return carry

    lax.fori_loop(0, NCH, start_a2a, 0)

    @pl.when(jnp.logical_not(has4))
    def _():
        ball[:, 4 * CH:5 * CH, :] = jnp.zeros((BAND, CH, LAG), jnp.bfloat16)

    @pl.when(jnp.logical_not(has2))
    def _():
        ball[:, 2 * CH:3 * CH, :] = jnp.zeros((BAND, CH, LAG), jnp.bfloat16)

    own_copy().wait()

    def block(d, k):
        return ball.at[pl.ds(FCH * k, FCH), pl.ds(CH * d, CH), :]

    def block_copy(src, d, k, target):
        return pltpu.make_async_remote_copy(
            src_ref=block(src, k), dst_ref=block(d, k),
            send_sem=blk_send.at[d - 1, k], recv_sem=blk_recv.at[d - 1, k],
            device_id=(target, me), device_id_type=MESH)

    def relayout(k):
        lane = lax.broadcasted_iota(jnp.int32, (2 * FCH, 128), 1)
        low = lane < 64
        even = lax.rem(lane // 32, 2) == 0

        def group(c4, carry):
            at = pl.ds(pl.multiple_of(c4 * 128, 128), 128)
            x = [rx[h, k, :, at].astype(jnp.float32) for h in range(SEG)]
            a0 = jnp.where(low, x[0], pltpu.roll(x[2], 64, 1))
            a2 = jnp.where(low, pltpu.roll(x[0], 64, 1), x[2])
            a1 = jnp.where(low, x[1], pltpu.roll(x[3], 64, 1))
            a3 = jnp.where(low, pltpu.roll(x[1], 64, 1), x[3])
            o0 = jnp.where(even, a0, pltpu.roll(a1, 32, 1))
            o1 = jnp.where(even, pltpu.roll(a0, 96, 1), a1)
            o2 = jnp.where(even, a2, pltpu.roll(a3, 32, 1))
            o3 = jnp.where(even, pltpu.roll(a2, 96, 1), a3)
            for c, o in enumerate((o0, o1, o2, o3)):
                rows = pl.ds(pl.multiple_of((c4 * 4 + c) * FCH, FCH), FCH)
                relay[0, rows, :] = o[:FCH]
                relay[1, rows, :] = o[FCH:]
            return carry

        lax.fori_loop(0, CH // 4, group, 0)
        for f in range(FCH):
            for p in range(2):
                v = relay[p, pl.ds(f, CH, stride=FCH), :]
                ball[FCH * k + f, 0:CH, 128 * p:128 * p + 128] = v.astype(jnp.bfloat16)

    def products(k, slot):
        def one_bin(f, carry):
            fi = FCH * k + f
            x = ball[fi, 0:CH, :]
            re = x[:, :128]
            im = x[:, 128:]
            left = jnp.concatenate(
                [x, jnp.concatenate([im, -re], axis=1)], axis=0)
            pr = lax.dot_general(left, ball[fi], (((1,), (1,)), ((), ())),
                                 preferred_element_type=jnp.float32) * SCALE
            pr = jnp.concatenate([pr, jnp.zeros((2 * CH, 64), jnp.float32)], axis=1)
            for q in range(2):
                half = pr[CH * q:CH * q + CH]
                row = lax.broadcasted_iota(jnp.int32, half.shape, 0)
                for bit in range(6):
                    moved = pltpu.roll(half, half.shape[1] - (1 << bit), 1)
                    half = jnp.where(lax.rem(row // (1 << bit), 2) == 1, moved, half)
                for t in range(LAG // 128):
                    prod[q, t, pl.ds(pl.multiple_of(f * CH, CH), CH), :] = half[:, 128 * t:128 * t + 128]
            return carry

        lax.fori_loop(0, FCH, one_bin, 0)

        def one_channel(c, carry):
            for q in range(2):
                for t in range(LAG // 128):
                    obuf[slot, c, q, :, 128 * t:128 * t + 128] = prod[
                        q, t, pl.ds(c, FCH, stride=CH), :]
            return carry

        lax.fori_loop(0, CH, one_channel, 0)

    def out_copy(k, slot):
        return pltpu.make_async_copy(
            obuf.at[slot], out_ref.at[:, :, pl.ds(FCH * k, FCH), :], out_sem.at[slot])

    def step(s, carry):
        @pl.when(s < NCH)
        def _():
            k = s
            for delta in (1, 2, 3):
                a2a_copy(delta, k).wait_recv()
            relayout(k)
            pl.when(to4)(lambda: block_copy(0, 4, k, chain - ROWY).start())
            pl.when(jnp.logical_not(first))(lambda: block_copy(0, 1, k, dst1).start())
            pl.when(last)(lambda: block_copy(0, 3, k, dst3).start())

        @pl.when(jnp.logical_and(s >= 2, s < NCH + 2))
        def _():
            k = s - 2
            pl.when(has4)(lambda: block_copy(0, 4, k, chain).wait_recv())
            pl.when(jnp.logical_not(last))(lambda: block_copy(4, 3, k, dst3).start())
            pl.when(first)(lambda: block_copy(4, 1, k, dst1).start())

        @pl.when(jnp.logical_and(s >= 3, s < NCH + 3))
        def _():
            k = s - 3
            block_copy(0, 1, k, dst1).wait_recv()
            pl.when(to2)(lambda: block_copy(1, 2, k, chain - 1).start())

        @pl.when(s >= 5)
        def _():
            k = s - 5
            slot = lax.rem(k, 2)
            block_copy(0, 3, k, dst3).wait_recv()
            pl.when(has2)(lambda: block_copy(1, 2, k, chain).wait_recv())
            pl.when(k >= 2)(lambda: out_copy(k - 2, slot).wait())
            products(k, slot)
            out_copy(k, slot).start()
        return carry

    lax.fori_loop(0, NCH + 5, step, 0)

    out_copy(NCH - 2, (NCH - 2) % 2).wait()
    out_copy(NCH - 1, (NCH - 1) % 2).wait()

    def drain(k, carry):
        for delta in (1, 2, 3):
            a2a_copy(delta, k).wait_send()
        pl.when(to4)(lambda: block_copy(0, 4, k, chain - ROWY).wait_send())
        block_copy(0, 1, k, dst1).wait_send()
        block_copy(0, 3, k, dst3).wait_send()
        pl.when(to2)(lambda: block_copy(1, 2, k, chain - 1).wait_send())
        return carry

    lax.fori_loop(0, NCH, drain, 0)


def per_device(traces):
    table = jnp.asarray(kernel_rows())
    dma = pltpu.SemaphoreType.DMA
    return pl.pallas_call(
        stack_kernel,
        out_shape=jax.ShapeDtypeStruct((CH, 2, BAND, LAG), jnp.float32),
        in_specs=[pl.BlockSpec(memory_space=pltpu.VMEM)] * 2,
        out_specs=pl.BlockSpec(memory_space=pl.ANY),
        scratch_shapes=[
            pltpu.VMEM((SEG, NCH, 2 * FCH, CH * WIN), jnp.bfloat16),
            pltpu.VMEM((SEG, NCH, 2 * FCH, CH * WIN), jnp.bfloat16),
            pltpu.VMEM((BAND, NBLK * CH, 2 * WIN * SEG), jnp.bfloat16),
            pltpu.VMEM((2, CH * FCH, 128), jnp.float32),
            pltpu.VMEM((2, LAG // 128, FCH * CH, 128), jnp.float32),
            pltpu.VMEM((2, CH, 2, FCH, LAG), jnp.float32),
            dma((3, NCH)), dma((3, NCH)), dma, dma((4, NCH)), dma((4, NCH)), dma((2,)),
        ],
        compiler_params=pltpu.CompilerParams(
            collective_id=0, has_side_effects=True, vmem_limit_bytes=48 << 20),
    )(traces, table)


def solution(mesh):
    return jax.shard_map(
        per_device,
        mesh=mesh,
        in_specs=(P("chain", "tm", None),),
        out_specs=P("chain", None, "tm", None),
        check_vma=False,
    )
```

```python
import math

import jax
import jax.numpy as jnp
import numpy as np
from jax import lax
from jax.experimental import pallas as pl
from jax.experimental.pallas import tpu as pltpu
from jax.sharding import PartitionSpec as P

MESH = pl.DeviceIdType.MESH
BF16 = jnp.bfloat16
F32 = jnp.float32

CH = 64
LAG = 256
BINS = 256
WIN = 32
NSAMP = 512
SEG = 4
BAND = BINS // SEG
FCH = 8
NCH = BAND // FCH
DEPTH = 2 * WIN * SEG
ROWY = 4
SCALE = 1.0 / math.sqrt(WIN * SEG)
FETCHED = ((), (2, 4, 6), (2, 4, 6), (2, 5))
FETCHED_FAR = ((), (2, 4, 6), (2, 4, 6), (2,5))
FETCHED_NEAR = (0,1,3,5,7)
AHEAD = 3
OWN_AT = (0, 2, 1)
TWO_AT = (4, 2, 1)
TWO_LAST_AT = (4, 2, 1)
PASS_AT = (2, 2, 1)
FOUR_AT = (2, 2, 1)
PAIRS_AT = (6, 2, 1)
FINISH_AT = (10, 2, 1)
FAR_LATE = 0


def tick_of(plan, k):
    offset, num, den = plan
    return offset + k * num // den


def chunk_at(plan, t, late=0):
    offset, num, den = plan
    offset = offset + late
    k = ((t - offset) * den + num - 1) // num
    fits = jnp.logical_and(t >= offset, k < NCH)
    return k, jnp.logical_and(fits, offset + k * num // den == t)


OWN, UP1, UP4, UP3, UP2 = 0, CH, 2 * CH, 3 * CH, 4 * CH


def kernel_rows():
    samples = np.arange(NSAMP, dtype=np.int32)
    freqs = np.arange(BINS, dtype=np.int32)
    phase = (samples[:, None] * freqs[None, :]) % NSAMP
    angles = np.float32(2.0 * math.pi / NSAMP) * phase.astype(np.float32)
    taper = np.float32(0.5) - np.float32(0.5) * np.cos(
        np.float32(2.0 * math.pi / NSAMP) * samples.astype(np.float32)
    )
    cosines = taper[:, None] * np.cos(angles)
    sines = -taper[:, None] * np.sin(angles)
    table = np.stack([cosines.T, sines.T], axis=0).astype(np.float32)
    table = table.reshape(2, SEG, NCH, FCH, NSAMP).transpose(1, 2, 0, 3, 4)
    return table.reshape(2 * BINS, NSAMP).astype(jnp.bfloat16)


def dot_nt(a, b):
    return lax.dot_general(a, b, (((1,), (1,)), ((), ())), preferred_element_type=F32)


def stack_kernel(tr_hbm, kt_hbm, out_ref, tr_ref, kt_ref, wt, rx, ball, lrev, osend, orecv,
                 stage, relay, prod, obuf, in_sem, a2a_send, a2a_recv, own_sem, blk_send, blk_recv,
                 hi_send, hi_recv, pass_send, stage_recv,
                 o_send, o_recv, out_sem):
    chain = lax.axis_index("chain")
    me = lax.axis_index("tm")
    n_chain = lax.axis_size("chain")
    y = lax.rem(chain, ROWY)

    cols = 256
    chans = cols // WIN
    n_in = CH // chans

    def in_copy(j):
        rows = pl.ds(chans * j, chans)
        return pltpu.make_async_copy(tr_hbm.at[rows], tr_ref.at[rows], in_sem.at[j])

    def table_copy():
        return pltpu.make_async_copy(kt_hbm, kt_ref, in_sem.at[n_in])

    table_copy().start()
    for j in range(n_in):
        in_copy(j).start()

    def peer(delta):
        return lax.rem(me + delta, SEG)

    def along(delta):
        return lax.rem(chain + n_chain + delta, n_chain)

    def bits(chunks):
        return sum(1 << k for k in chunks)

    def fetched_set(i):
        place = lax.rem(i, ROWY)
        depth = lax.rem(i // ROWY, ROWY)
        mask = jnp.int32(0)
        for p in range(ROWY):
            there = place == p
            mask = jnp.where(there, bits(FETCHED[p]), mask)
            mask = jnp.where(jnp.logical_and(there, depth == ROWY - 1),
                             bits(FETCHED_FAR[p]), mask)
        return jnp.where(jnp.logical_and(place == 0, depth == 0), bits(FETCHED_NEAR), mask)

    here, below, above = chain, along(-1), along(1)
    fetched_sets = [(i, fetched_set(i)) for i in (here, below, above, 0)]

    def is_fetched(i, k):
        mask = [m for j, m in fetched_sets if j is i][0]
        return lax.rem(lax.shift_right_logical(mask, jnp.int32(k)), 2) == 1

    def paired(i, k):
        return jnp.logical_not(is_fetched(i, k))

    def gets1(i, k):
        return jnp.logical_or(i + 1 < n_chain, paired(0, k))

    def gets2(i, k):
        return jnp.logical_and(i + 2 < n_chain, is_fetched(i, k))

    def gets3(i, k):
        return jnp.logical_or(i + 3 < n_chain, jnp.logical_and(i == n_chain - 1, paired(0, k)))

    def gets4(i, k):
        extra = jnp.logical_or(i == n_chain - 4, i == n_chain - 2)
        return jnp.logical_or(i + 4 < n_chain, jnp.logical_and(extra, paired(0, k)))

    def gets_pairs(i, k):
        return jnp.logical_and(i + 2 < n_chain, paired(i, k))

    first = y == 0
    last = y == ROWY - 1
    src1 = jnp.where(last, chain - (ROWY - 1), chain + 1)
    src3 = jnp.where(first, chain + (ROWY - 1), chain - 1)
    dst1 = jnp.where(first, chain + (ROWY - 1), chain - 1)
    dst3 = jnp.where(last, chain - (ROWY - 1), chain + 1)

    barrier = pltpu.get_barrier_semaphore()

    def greet(c, t):
        pl.semaphore_signal(barrier, inc=1, device_id=(c, t), device_id_type=MESH)

    for delta in (1, 2, 3):
        greet(chain, peer(delta))
    for source in (src1, src3, along(ROWY), along(1), along(-1)):
        greet(source, me)
    greet(along(-3 * ROWY), me)
    greet(along(n_chain // 2), me)

    table_copy().wait()

    def whiten(j, carry):
        in_copy(j).wait()
        tr = tr_ref[pl.ds(chans * j, chans)].reshape(cols, NSAMP)
        spec = dot_nt(kt_ref[...], tr).reshape(SEG * NCH, 2, FCH, cols)
        re = spec[:, 0]
        im = spec[:, 1]
        mag = jnp.sqrt(re * re + im * im)
        level = jnp.sum(mag, axis=(0, 1), keepdims=True) * (1.0 / BINS)
        inv = 1.0 / (mag + 0.1 * (level + 1e-6))
        white = jnp.stack([re * inv, im * inv], axis=1)
        white = white.reshape(SEG, NCH, 2 * FCH, cols).astype(BF16)
        wt[:, :, :, pl.ds(pl.multiple_of(cols * j, cols), cols)] = white
        return carry

    lax.fori_loop(0, n_in, whiten, 0)

    pl.semaphore_wait(barrier, 10)

    def a2a_copy(delta, k):
        return pltpu.make_async_remote_copy(
            src_ref=wt.at[peer(delta), k], dst_ref=rx.at[me, k],
            send_sem=a2a_send.at[delta - 1, k], recv_sem=a2a_recv.at[delta - 1, k],
            device_id=(chain, peer(delta)), device_id_type=MESH)

    def own_copy():
        return pltpu.make_async_copy(wt.at[me], rx.at[me], own_sem)

    own_copy().start()

    def start_a2a(k, carry):
        for delta in (1, 2, 3):
            a2a_copy(delta, k).start()
        return carry

    lax.fori_loop(0, AHEAD, start_a2a, 0)
    own_copy().wait()

    def block(rows, k):
        return ball.at[pl.ds(FCH * k, FCH), pl.ds(rows, CH), :]

    def block_copy(src, dst, k, target):
        return pltpu.make_async_remote_copy(
            src_ref=block(src, k), dst_ref=block(dst, k),
            send_sem=blk_send.at[dst // CH - 1, k], recv_sem=blk_recv.at[dst // CH - 1, k],
            device_id=(target, me), device_id_type=MESH)

    HALF = FCH // 2
    depth = lax.rem(chain // ROWY, ROWY)
    upper = chain >= n_chain // 2
    far_from = jnp.logical_and(upper, depth == 0)
    passes = jnp.logical_and(upper, depth == ROWY - 1)
    far_to = depth == ROWY - 1

    def half_copy(src, dst, send, recv, target):
        return pltpu.make_async_remote_copy(
            src_ref=src, dst_ref=dst, send_sem=send, recv_sem=recv,
            device_id=target, device_id_type=MESH)

    def bins_of(rows, k, half):
        return ball.at[pl.ds(FCH * k + HALF * half, HALF), pl.ds(rows, CH), :]

    def low4(k, target):
        return half_copy(bins_of(OWN, k, 0), bins_of(UP4, k, 0),
                         blk_send.at[1, k], blk_recv.at[1, k], (target, me))

    def high4(k, target):
        return half_copy(bins_of(OWN, k, 1), bins_of(UP4, k, 1),
                         hi_send.at[k], hi_recv.at[k], (target, me))

    def stage4(k):
        return half_copy(bins_of(OWN, k, 1), stage.at[k],
                         hi_send.at[k], stage_recv.at[k], (along(3 * ROWY), me))

    def pass4(k):
        return half_copy(stage.at[k], bins_of(UP4, k, 1),
                         pass_send.at[k], hi_recv.at[k], (along(n_chain // 2), me))

    def product_copy(k):
        bins = pl.ds(FCH * k, FCH)
        return pltpu.make_async_remote_copy(
            src_ref=osend.at[bins], dst_ref=orecv.at[bins],
            send_sem=o_send.at[k], recv_sem=o_recv.at[k],
            device_id=(along(1), me), device_id_type=MESH)

    rows64 = lax.broadcasted_iota(jnp.int32, (CH, CH), 0)
    cols64 = lax.broadcasted_iota(jnp.int32, (CH, CH), 1)
    flip = (rows64 + cols64 == CH - 1).astype(F32).astype(BF16)

    def flipped(x):
        return jnp.dot(flip, x, preferred_element_type=F32).astype(BF16)

    def relayout(k):
        lane = lax.broadcasted_iota(jnp.int32, (2 * FCH, 128), 1)
        low = lane < 64
        even = lax.rem(lane // 32, 2) == 0

        def group(c4):
            at = pl.ds(pl.multiple_of(c4 * 128, 128), 128)
            x = [rx[h, k, :, at].astype(F32) for h in range(SEG)]
            a0 = jnp.where(low, x[0], pltpu.roll(x[2], 64, 1))
            a2 = jnp.where(low, pltpu.roll(x[0], 64, 1), x[2])
            a1 = jnp.where(low, x[1], pltpu.roll(x[3], 64, 1))
            a3 = jnp.where(low, pltpu.roll(x[1], 64, 1), x[3])
            o0 = jnp.where(even, a0, pltpu.roll(a1, 32, 1))
            o1 = jnp.where(even, pltpu.roll(a0, 96, 1), a1)
            o2 = jnp.where(even, a2, pltpu.roll(a3, 32, 1))
            o3 = jnp.where(even, pltpu.roll(a2, 96, 1), a3)
            for c, o in enumerate((o0, o1, o2, o3)):
                rows = pl.ds(pl.multiple_of((c4 * 4 + c) * FCH, FCH), FCH)
                relay[0, rows, :] = o[:FCH]
                relay[1, rows, :] = o[FCH:]

        def groups(i, carry):
            for u in range(4):
                group(i * 4 + u)
            return carry

        lax.fori_loop(0, CH // 16, groups, 0)
        for f in range(FCH):
            halves = [relay[p, pl.ds(f, CH, stride=FCH), :] for p in range(2)]
            x = jnp.concatenate(halves, axis=1).astype(BF16)
            ball[FCH * k + f, OWN:OWN + CH, :] = x
            lrev[FCH * k + f] = flipped(x)

    def neighbour_products(k):
        def bins(i, carry):
            for u in range(4):
                fi = FCH * k + i * 4 + u
                left = flipped(ball[fi, UP1:UP1 + CH, :])
                right = ball[fi, UP3:UP3 + CH, :]
                turned = jnp.concatenate([-right[:, 128:], right[:, :128]], axis=1)
                both = jnp.concatenate([right, turned], axis=0)
                osend[fi] = dot_nt(left, both).astype(BF16)
            return carry

        lax.fori_loop(0, FCH // 4, bins, 0)

    lane = lax.broadcasted_iota(jnp.int32, (CH, 128), 1)
    low = lane < 64
    lane3 = lax.broadcasted_iota(jnp.int32, (1, 384), 1)
    inside = (chain + lane3 // CH) < n_chain

    def products(k, slot, fetched):
        def one_bin(f):
            fi = FCH * k + f
            x = lrev[fi]
            turned = jnp.concatenate([x[:, 128:], -x[:, :128]], axis=1)
            left = jnp.concatenate([x, turned], axis=0)
            if fetched:
                pr = dot_nt(left, ball[fi])
                pad = jnp.zeros((2 * CH, 64), F32)
                two = jnp.concatenate([pr[:, 256:], pad], axis=1)
                two = [two[:CH], two[CH:]]
            else:
                pr = dot_nt(left, ball[fi, :256, :])
                o = orecv[fi].astype(F32)
                two = [o, pltpu.roll(o, 64, 1)]
            for q in range(2):
                p0 = pr[CH * q:CH * q + CH, :128]
                p1 = pr[CH * q:CH * q + CH, 128:256]
                mid = jnp.where(low, two[q], p1)
                full = jnp.concatenate([p0, mid, p1], axis=1) * SCALE
                full = jnp.where(inside, full, 0.0)
                full = pltpu.roll(full, 384 - (CH - 1), 1, stride=1, stride_axis=0)
                for t in range(LAG // 128):
                    prod[q, t, pl.ds(f * CH, CH), :] = full[:, 128 * t:128 * t + 128]

        for f in range(FCH):
            one_bin(f)

    def to_rows(slot):
        def channels(i, carry):
            for u in range(16):
                c = i * 16 + u
                for q in range(2):
                    for t in range(LAG // 128):
                        obuf[slot, c, FCH * q:FCH * q + FCH, 128 * t:128 * t + 128] = prod[
                            q, t, pl.ds(CH - 1 - c, FCH, stride=CH), :].astype(BF16)
            return carry

        lax.fori_loop(0, CH // 16, channels, 0)

    def out_copy(k, slot):
        return pltpu.make_async_copy(
            obuf.at[slot], out_ref.at[k], out_sem.at[slot])

    def both(a, b):
        return jnp.logical_and(a, b)

    send1_own = jnp.logical_not(first)
    send3_own = last

    late = jnp.where(far_to, FAR_LATE, 0)

    def send_two(k):
        pl.when(gets1(chain, k))(lambda: block_copy(OWN, UP1, k, dst1).wait_recv())
        pl.when(gets2(below, k))(
            lambda: block_copy(UP1, UP2, k, along(-1)).start())

    def step(t, carry):
        k_own, now = chunk_at(OWN_AT, t)

        @pl.when(now)
        def _():
            k = k_own
            for delta in (1, 2, 3):
                a2a_copy(delta, k).wait_recv()
            pl.when(k + AHEAD < NCH)(lambda: start_a2a(k + AHEAD, None))
            relayout(k)

            @pl.when(gets4(along(-ROWY), k))
            def _():
                low4(k, along(-ROWY)).start()
                pl.when(far_from)(lambda: stage4(k).start())
                pl.when(jnp.logical_not(far_from))(lambda: high4(k, along(-ROWY)).start())

            pl.when(both(send1_own, gets1(dst1, k)))(
                lambda: block_copy(OWN, UP1, k, dst1).start())
            pl.when(both(send3_own, gets3(dst3, k)))(
                lambda: block_copy(OWN, UP3, k, dst3).start())

        k_two, now = chunk_at(TWO_AT, t)

        @pl.when(both(jnp.logical_not(last), now))
        def _():
            send_two(k_two)

        k_pass, now = chunk_at(PASS_AT, t, late)

        @pl.when(both(passes, now))
        def _():
            k = k_pass

            stage4(k).wait_recv()
            pass4(k).start()

        k_four, now = chunk_at(FOUR_AT, t, late)

        @pl.when(now)
        def _():
            k = k_four

            @pl.when(gets4(chain, k))
            def _():
                low4(k, chain).wait_recv()
                high4(k, chain).wait_recv()

            pl.when(both(jnp.logical_not(send3_own), gets3(dst3, k)))(
                lambda: block_copy(UP4, UP3, k, dst3).start())
            pl.when(both(jnp.logical_not(send1_own), gets1(dst1, k)))(
                lambda: block_copy(UP4, UP1, k, dst1).start())

        k_last, now = chunk_at(TWO_LAST_AT, t, late)

        @pl.when(both(last, now))
        def _():
            send_two(k_last)

        k_pairs, now = chunk_at(PAIRS_AT, t, late)

        @pl.when(now)
        def _():
            k = k_pairs
            pl.when(gets3(chain, k))(lambda: block_copy(OWN, UP3, k, dst3).wait_recv())

            @pl.when(gets_pairs(above, k))
            def _():
                neighbour_products(k)
                product_copy(k).start()

        k_finish, now = chunk_at(FINISH_AT, t, late)

        @pl.when(now)
        def _():
            k = k_finish
            slot = lax.rem(k, 2)
            pl.when(k >= 2)(lambda: out_copy(k - 2, slot).wait())
            pl.when(gets2(chain, k))(lambda: block_copy(UP1, UP2, k, chain).wait_recv())
            pl.when(gets_pairs(chain, k))(lambda: product_copy(k).wait_recv())
            pl.when(is_fetched(chain, k))(lambda: products(k, slot, True))
            pl.when(paired(chain, k))(lambda: products(k, slot, False))
            to_rows(slot)
            out_copy(k, slot).start()
        return carry

    lax.fori_loop(0, tick_of(FINISH_AT, NCH - 1) + 1 + FAR_LATE, step, 0)

    out_copy(NCH - 2, (NCH - 2) % 2).wait()
    out_copy(NCH - 1, (NCH - 1) % 2).wait()

    def drain(k, carry):
        for delta in (1, 2, 3):
            a2a_copy(delta, k).wait_send()

        @pl.when(gets4(along(-ROWY), k))
        def _():
            low4(k, along(-ROWY)).wait_send()
            high4(k, along(-ROWY)).wait_send()

        pl.when(passes)(lambda: pass4(k).wait_send())
        pl.when(gets1(dst1, k))(lambda: block_copy(OWN, UP1, k, dst1).wait_send())
        pl.when(gets3(dst3, k))(lambda: block_copy(OWN, UP3, k, dst3).wait_send())
        pl.when(gets2(below, k))(
            lambda: block_copy(UP1, UP2, k, along(-1)).wait_send())
        pl.when(gets_pairs(above, k))(lambda: product_copy(k).wait_send())
        return carry

    lax.fori_loop(0, NCH, drain, 0)


def widen_kernel(in_ref, out_ref):
    for k in range(NCH):
        for q in range(2):
            out_ref[:, q, FCH * k:FCH * k + FCH, :] = in_ref[
                k, :, FCH * q:FCH * q + FCH, :].astype(F32)


def per_device(traces):
    table = jnp.asarray(kernel_rows())
    dma = pltpu.SemaphoreType.DMA
    hbm = pl.BlockSpec(memory_space=pltpu.MemorySpace.HBM)
    stacks = pl.pallas_call(
        stack_kernel,
        out_shape=jax.ShapeDtypeStruct((NCH, CH, 2 * FCH, LAG), BF16),
        in_specs=[hbm, hbm],
        out_specs=hbm,
        scratch_shapes=[
            pltpu.VMEM((CH, WIN, NSAMP), BF16),
            pltpu.VMEM((2 * BINS, NSAMP), BF16),
            pltpu.VMEM((SEG, NCH, 2 * FCH, CH * WIN), BF16),
            pltpu.VMEM((SEG, NCH, 2 * FCH, CH * WIN), BF16),
            pltpu.VMEM((BAND, 5 * CH, DEPTH), BF16),
            pltpu.VMEM((BAND, CH, DEPTH), BF16),
            pltpu.VMEM((BAND, CH, 2 * CH), BF16),
            pltpu.VMEM((BAND, CH, 2 * CH), BF16),
            pltpu.VMEM((NCH, FCH // 2, CH, DEPTH), BF16),
            pltpu.VMEM((2, CH * FCH, 128), F32),
            pltpu.VMEM((2, LAG // 128, FCH * CH, 128), F32),
            pltpu.VMEM((2, CH, 2 * FCH, LAG), BF16),
            dma((9,)), dma((3, NCH)), dma((3, NCH)), dma, dma((4, NCH)), dma((4, NCH)),
            dma((NCH,)), dma((NCH,)), dma((NCH,)), dma((NCH,)),
            dma((NCH,)), dma((NCH,)), dma((2,)),
        ],
        compiler_params=pltpu.CompilerParams(
            collective_id=0, has_side_effects=True, vmem_limit_bytes=48 << 20),
    )(traces, table)
    part = 16
    return pl.pallas_call(
        widen_kernel,
        grid=(CH // part,),
        out_shape=jax.ShapeDtypeStruct((CH, 2, BAND, LAG), F32),
        in_specs=[pl.BlockSpec((NCH, part, 2 * FCH, LAG), lambda i: (0, i, 0, 0))],
        out_specs=pl.BlockSpec((part, 2, BAND, LAG), lambda i: (i, 0, 0, 0)),
    )(stacks)


def solution(mesh):
    return jax.shard_map(
        per_device,
        mesh=mesh,
        in_specs=(P("chain", "tm", None),),
        out_specs=P("chain", None, "tm", None),
        check_vma=False,
    )
```

```python
import math

import jax
import jax.numpy as jnp
import numpy as np
from jax import lax
from jax.experimental import pallas as pl
from jax.experimental.pallas import tpu as pltpu
from jax.sharding import PartitionSpec as P

MESH = pl.DeviceIdType.MESH
BF16 = jnp.bfloat16
F32 = jnp.float32

CH = 64
LAG = 256
BINS = 256
WIN = 32
NSAMP = 512
SEG = 4
BAND = BINS // SEG
FCH = 8
NCH = BAND // FCH
DEPTH = 2 * WIN * SEG
ROWY = 4
SCALE = 1.0 / math.sqrt(WIN * SEG)
FETCHED = ((), (2, 5), (2, 5), (3,))
FETCHED_FAR = ((), (2, 4, 6), (2, 4, 6), (2,5))
FETCHED_NEAR = (0,1,3,5,7)
AHEAD = 3
OWN_AT = (0, 2, 1)
TWO_AT = (4, 2, 1)
TWO_LAST_AT = (4, 2, 1)
PASS_AT = (2, 2, 1)
FOUR_AT = (2, 2, 1)
PAIRS_AT = (6, 2, 1)
FINISH_AT = (10, 2, 1)
FAR_LATE = 0


def tick_of(plan, k):
    offset, num, den = plan
    return offset + k * num // den


def chunk_at(plan, t, late=0):
    offset, num, den = plan
    offset = offset + late
    k = ((t - offset) * den + num - 1) // num
    fits = jnp.logical_and(t >= offset, k < NCH)
    return k, jnp.logical_and(fits, offset + k * num // den == t)


OWN, UP1, UP4, UP3, UP2 = 0, CH, 2 * CH, 3 * CH, 4 * CH


def kernel_rows():
    samples = np.arange(NSAMP, dtype=np.int32)
    freqs = np.arange(BINS, dtype=np.int32)
    phase = (samples[:, None] * freqs[None, :]) % NSAMP
    angles = np.float32(2.0 * math.pi / NSAMP) * phase.astype(np.float32)
    taper = np.float32(0.5) - np.float32(0.5) * np.cos(
        np.float32(2.0 * math.pi / NSAMP) * samples.astype(np.float32)
    )
    cosines = taper[:, None] * np.cos(angles)
    sines = -taper[:, None] * np.sin(angles)
    table = np.stack([cosines.T, sines.T], axis=0).astype(np.float32)
    table = table.reshape(2, SEG, NCH, FCH, NSAMP).transpose(1, 2, 0, 3, 4)
    return table.reshape(2 * BINS, NSAMP).astype(jnp.bfloat16)


def dot_nt(a, b):
    return lax.dot_general(a, b, (((1,), (1,)), ((), ())), preferred_element_type=F32)


def stack_kernel(tr_hbm, kt_hbm, out_ref, tr_ref, kt_ref, wt, rx, ball, lrev, osend, orecv,
                 stage, relay, prod, obuf, in_sem, a2a_send, a2a_recv, own_sem, blk_send, blk_recv,
                 hi_send, hi_recv, pass_send, stage_recv,
                 o_send, o_recv, out_sem):
    chain = lax.axis_index("chain")
    me = lax.axis_index("tm")
    n_chain = lax.axis_size("chain")
    y = lax.rem(chain, ROWY)

    cols = 256
    chans = cols // WIN
    n_in = CH // chans

    def in_copy(j):
        rows = pl.ds(chans * j, chans)
        return pltpu.make_async_copy(tr_hbm.at[rows], tr_ref.at[rows], in_sem.at[j])

    def table_copy():
        return pltpu.make_async_copy(kt_hbm, kt_ref, in_sem.at[n_in])

    table_copy().start()
    for j in range(n_in):
        in_copy(j).start()

    def peer(delta):
        return lax.rem(me + delta, SEG)

    def along(delta):
        return lax.rem(chain + n_chain + delta, n_chain)

    def bits(chunks):
        return sum(1 << k for k in chunks)

    def fetched_set(i):
        place = lax.rem(i, ROWY)
        depth = lax.rem(i // ROWY, ROWY)
        mask = jnp.int32(0)
        for p in range(ROWY):
            there = place == p
            mask = jnp.where(there, bits(FETCHED[p]), mask)
            mask = jnp.where(jnp.logical_and(there, depth == ROWY - 1),
                             bits(FETCHED_FAR[p]), mask)
        return jnp.where(jnp.logical_and(place == 0, depth == 0), bits(FETCHED_NEAR), mask)

    here, below, above = chain, along(-1), along(1)
    fetched_sets = [(i, fetched_set(i)) for i in (here, below, above, 0)]

    def is_fetched(i, k):
        mask = [m for j, m in fetched_sets if j is i][0]
        return lax.rem(lax.shift_right_logical(mask, jnp.int32(k)), 2) == 1

    def paired(i, k):
        return jnp.logical_not(is_fetched(i, k))

    def gets1(i, k):
        return jnp.logical_or(i + 1 < n_chain, paired(0, k))

    def gets2(i, k):
        return jnp.logical_and(i + 2 < n_chain, is_fetched(i, k))

    def gets3(i, k):
        return jnp.logical_or(i + 3 < n_chain, jnp.logical_and(i == n_chain - 1, paired(0, k)))

    def gets4(i, k):
        extra = jnp.logical_or(i == n_chain - 4, i == n_chain - 2)
        return jnp.logical_or(i + 4 < n_chain, jnp.logical_and(extra, paired(0, k)))

    def gets_pairs(i, k):
        return jnp.logical_and(i + 2 < n_chain, paired(i, k))

    first = y == 0
    last = y == ROWY - 1
    src1 = jnp.where(last, chain - (ROWY - 1), chain + 1)
    src3 = jnp.where(first, chain + (ROWY - 1), chain - 1)
    dst1 = jnp.where(first, chain + (ROWY - 1), chain - 1)
    dst3 = jnp.where(last, chain - (ROWY - 1), chain + 1)

    barrier = pltpu.get_barrier_semaphore()

    def greet(c, t):
        pl.semaphore_signal(barrier, inc=1, device_id=(c, t), device_id_type=MESH)

    for delta in (1, 2, 3):
        greet(chain, peer(delta))
    for source in (src1, src3, along(ROWY), along(1), along(-1)):
        greet(source, me)
    greet(along(-3 * ROWY), me)
    greet(along(n_chain // 2), me)

    table_copy().wait()

    def whiten(j, carry):
        in_copy(j).wait()
        tr = tr_ref[pl.ds(chans * j, chans)].reshape(cols, NSAMP)
        spec = dot_nt(kt_ref[...], tr).reshape(SEG * NCH, 2, FCH, cols)
        re = spec[:, 0]
        im = spec[:, 1]
        mag = jnp.sqrt(re * re + im * im)
        level = jnp.sum(mag, axis=(0, 1), keepdims=True) * (1.0 / BINS)
        inv = 1.0 / (mag + 0.1 * (level + 1e-6))
        white = jnp.stack([re * inv, im * inv], axis=1)
        white = white.reshape(SEG, NCH, 2 * FCH, cols).astype(BF16)
        wt[:, :, :, pl.ds(pl.multiple_of(cols * j, cols), cols)] = white
        return carry

    lax.fori_loop(0, n_in, whiten, 0)

    pl.semaphore_wait(barrier, 10)

    def a2a_copy(delta, k):
        return pltpu.make_async_remote_copy(
            src_ref=wt.at[peer(delta), k], dst_ref=rx.at[me, k],
            send_sem=a2a_send.at[delta - 1, k], recv_sem=a2a_recv.at[delta - 1, k],
            device_id=(chain, peer(delta)), device_id_type=MESH)

    def own_copy():
        return pltpu.make_async_copy(wt.at[me], rx.at[me], own_sem)

    own_copy().start()

    def start_a2a(k, carry):
        for delta in (1, 2, 3):
            a2a_copy(delta, k).start()
        return carry

    lax.fori_loop(0, AHEAD, start_a2a, 0)
    own_copy().wait()

    def block(rows, k):
        return ball.at[pl.ds(FCH * k, FCH), pl.ds(rows, CH), :]

    def block_copy(src, dst, k, target):
        return pltpu.make_async_remote_copy(
            src_ref=block(src, k), dst_ref=block(dst, k),
            send_sem=blk_send.at[dst // CH - 1, k], recv_sem=blk_recv.at[dst // CH - 1, k],
            device_id=(target, me), device_id_type=MESH)

    HALF = FCH // 2
    depth = lax.rem(chain // ROWY, ROWY)
    upper = chain >= n_chain // 2
    far_from = jnp.logical_and(upper, depth == 0)
    passes = jnp.logical_and(upper, depth == ROWY - 1)
    far_to = depth == ROWY - 1

    def half_copy(src, dst, send, recv, target):
        return pltpu.make_async_remote_copy(
            src_ref=src, dst_ref=dst, send_sem=send, recv_sem=recv,
            device_id=target, device_id_type=MESH)

    def bins_of(rows, k, half):
        return ball.at[pl.ds(FCH * k + HALF * half, HALF), pl.ds(rows, CH), :]

    def low4(k, target):
        return half_copy(bins_of(OWN, k, 0), bins_of(UP4, k, 0),
                         blk_send.at[1, k], blk_recv.at[1, k], (target, me))

    def high4(k, target):
        return half_copy(bins_of(OWN, k, 1), bins_of(UP4, k, 1),
                         hi_send.at[k], hi_recv.at[k], (target, me))

    def stage4(k):
        return half_copy(bins_of(OWN, k, 1), stage.at[k],
                         hi_send.at[k], stage_recv.at[k], (along(3 * ROWY), me))

    def pass4(k):
        return half_copy(stage.at[k], bins_of(UP4, k, 1),
                         pass_send.at[k], hi_recv.at[k], (along(n_chain // 2), me))

    def product_copy(k):
        bins = pl.ds(FCH * k, FCH)
        return pltpu.make_async_remote_copy(
            src_ref=osend.at[bins], dst_ref=orecv.at[bins],
            send_sem=o_send.at[k], recv_sem=o_recv.at[k],
            device_id=(along(1), me), device_id_type=MESH)

    rows64 = lax.broadcasted_iota(jnp.int32, (CH, CH), 0)
    cols64 = lax.broadcasted_iota(jnp.int32, (CH, CH), 1)
    flip = (rows64 + cols64 == CH - 1).astype(F32).astype(BF16)

    def flipped(x):
        return jnp.dot(flip, x, preferred_element_type=F32).astype(BF16)

    def relayout(k):
        lane = lax.broadcasted_iota(jnp.int32, (2 * FCH, 128), 1)
        low = lane < 64
        even = lax.rem(lane // 32, 2) == 0

        def group(c4):
            at = pl.ds(pl.multiple_of(c4 * 128, 128), 128)
            x = [rx[h, k, :, at].astype(F32) for h in range(SEG)]
            a0 = jnp.where(low, x[0], pltpu.roll(x[2], 64, 1))
            a2 = jnp.where(low, pltpu.roll(x[0], 64, 1), x[2])
            a1 = jnp.where(low, x[1], pltpu.roll(x[3], 64, 1))
            a3 = jnp.where(low, pltpu.roll(x[1], 64, 1), x[3])
            o0 = jnp.where(even, a0, pltpu.roll(a1, 32, 1))
            o1 = jnp.where(even, pltpu.roll(a0, 96, 1), a1)
            o2 = jnp.where(even, a2, pltpu.roll(a3, 32, 1))
            o3 = jnp.where(even, pltpu.roll(a2, 96, 1), a3)
            for c, o in enumerate((o0, o1, o2, o3)):
                rows = pl.ds(pl.multiple_of((c4 * 4 + c) * FCH, FCH), FCH)
                relay[0, rows, :] = o[:FCH]
                relay[1, rows, :] = o[FCH:]

        def groups(i, carry):
            for u in range(4):
                group(i * 4 + u)
            return carry

        lax.fori_loop(0, CH // 16, groups, 0)
        for f in range(FCH):
            halves = [relay[p, pl.ds(f, CH, stride=FCH), :] for p in range(2)]
            x = jnp.concatenate(halves, axis=1).astype(BF16)
            ball[FCH * k + f, OWN:OWN + CH, :] = x
            lrev[FCH * k + f] = flipped(x)

    def neighbour_products(k):
        def bins(i, carry):
            for u in range(4):
                fi = FCH * k + i * 4 + u
                left = flipped(ball[fi, UP1:UP1 + CH, :])
                right = ball[fi, UP3:UP3 + CH, :]
                turned = jnp.concatenate([-right[:, 128:], right[:, :128]], axis=1)
                both = jnp.concatenate([right, turned], axis=0)
                osend[fi] = dot_nt(left, both).astype(BF16)
            return carry

        lax.fori_loop(0, FCH // 4, bins, 0)

    lane = lax.broadcasted_iota(jnp.int32, (CH, 128), 1)
    low = lane < 64
    lane3 = lax.broadcasted_iota(jnp.int32, (1, 384), 1)
    inside = (chain + lane3 // CH) < n_chain

    def products(k, slot, fetched):
        def one_bin(f):
            fi = FCH * k + f
            x = lrev[fi]
            turned = jnp.concatenate([x[:, 128:], -x[:, :128]], axis=1)
            left = jnp.concatenate([x, turned], axis=0)
            if fetched:
                pr = dot_nt(left, ball[fi])
                pad = jnp.zeros((2 * CH, 64), F32)
                two = jnp.concatenate([pr[:, 256:], pad], axis=1)
                two = [two[:CH], two[CH:]]
            else:
                pr = dot_nt(left, ball[fi, :256, :])
                o = orecv[fi].astype(F32)
                two = [o, pltpu.roll(o, 64, 1)]
            for q in range(2):
                p0 = pr[CH * q:CH * q + CH, :128]
                p1 = pr[CH * q:CH * q + CH, 128:256]
                mid = jnp.where(low, two[q], p1)
                full = jnp.concatenate([p0, mid, p1], axis=1) * SCALE
                full = jnp.where(inside, full, 0.0)
                full = pltpu.roll(full, 384 - (CH - 1), 1, stride=1, stride_axis=0)
                for t in range(LAG // 128):
                    prod[q, t, pl.ds(f * CH, CH), :] = full[:, 128 * t:128 * t + 128]

        for f in range(FCH):
            one_bin(f)

    def to_rows(slot):
        def channels(i, carry):
            for u in range(16):
                c = i * 16 + u
                for q in range(2):
                    for t in range(LAG // 128):
                        obuf[slot, c, FCH * q:FCH * q + FCH, 128 * t:128 * t + 128] = prod[
                            q, t, pl.ds(CH - 1 - c, FCH, stride=CH), :].astype(BF16)
            return carry

        lax.fori_loop(0, CH // 16, channels, 0)

    def out_copy(k, slot):
        return pltpu.make_async_copy(
            obuf.at[slot], out_ref.at[k], out_sem.at[slot])

    def both(a, b):
        return jnp.logical_and(a, b)

    send1_own = jnp.logical_not(first)
    send3_own = last

    late = jnp.where(far_to, FAR_LATE, 0)

    def send_two(k):
        pl.when(gets1(chain, k))(lambda: block_copy(OWN, UP1, k, dst1).wait_recv())
        pl.when(gets2(below, k))(
            lambda: block_copy(UP1, UP2, k, along(-1)).start())

    def step(t, carry):
        k_own, now = chunk_at(OWN_AT, t)

        @pl.when(now)
        def _():
            k = k_own
            for delta in (1, 2, 3):
                a2a_copy(delta, k).wait_recv()
            pl.when(k + AHEAD < NCH)(lambda: start_a2a(k + AHEAD, None))
            relayout(k)

            @pl.when(gets4(along(-ROWY), k))
            def _():
                low4(k, along(-ROWY)).start()
                pl.when(far_from)(lambda: stage4(k).start())
                pl.when(jnp.logical_not(far_from))(lambda: high4(k, along(-ROWY)).start())

            pl.when(both(send1_own, gets1(dst1, k)))(
                lambda: block_copy(OWN, UP1, k, dst1).start())
            pl.when(both(send3_own, gets3(dst3, k)))(
                lambda: block_copy(OWN, UP3, k, dst3).start())

        k_two, now = chunk_at(TWO_AT, t)

        @pl.when(both(jnp.logical_not(last), now))
        def _():
            send_two(k_two)

        k_pass, now = chunk_at(PASS_AT, t, late)

        @pl.when(both(passes, now))
        def _():
            k = k_pass

            stage4(k).wait_recv()
            pass4(k).start()

        k_four, now = chunk_at(FOUR_AT, t, late)

        @pl.when(now)
        def _():
            k = k_four

            @pl.when(gets4(chain, k))
            def _():
                low4(k, chain).wait_recv()
                high4(k, chain).wait_recv()

            pl.when(both(jnp.logical_not(send3_own), gets3(dst3, k)))(
                lambda: block_copy(UP4, UP3, k, dst3).start())
            pl.when(both(jnp.logical_not(send1_own), gets1(dst1, k)))(
                lambda: block_copy(UP4, UP1, k, dst1).start())

        k_last, now = chunk_at(TWO_LAST_AT, t, late)

        @pl.when(both(last, now))
        def _():
            send_two(k_last)

        k_pairs, now = chunk_at(PAIRS_AT, t, late)

        @pl.when(now)
        def _():
            k = k_pairs
            pl.when(gets3(chain, k))(lambda: block_copy(OWN, UP3, k, dst3).wait_recv())

            @pl.when(gets_pairs(above, k))
            def _():
                neighbour_products(k)
                product_copy(k).start()

        k_finish, now = chunk_at(FINISH_AT, t, late)

        @pl.when(now)
        def _():
            k = k_finish
            slot = lax.rem(k, 2)
            pl.when(k >= 2)(lambda: out_copy(k - 2, slot).wait())
            pl.when(gets2(chain, k))(lambda: block_copy(UP1, UP2, k, chain).wait_recv())
            pl.when(gets_pairs(chain, k))(lambda: product_copy(k).wait_recv())
            pl.when(is_fetched(chain, k))(lambda: products(k, slot, True))
            pl.when(paired(chain, k))(lambda: products(k, slot, False))
            to_rows(slot)
            out_copy(k, slot).start()
        return carry

    lax.fori_loop(0, tick_of(FINISH_AT, NCH - 1) + 1 + FAR_LATE, step, 0)

    out_copy(NCH - 2, (NCH - 2) % 2).wait()
    out_copy(NCH - 1, (NCH - 1) % 2).wait()

    def drain(k, carry):
        for delta in (1, 2, 3):
            a2a_copy(delta, k).wait_send()

        @pl.when(gets4(along(-ROWY), k))
        def _():
            low4(k, along(-ROWY)).wait_send()
            high4(k, along(-ROWY)).wait_send()

        pl.when(passes)(lambda: pass4(k).wait_send())
        pl.when(gets1(dst1, k))(lambda: block_copy(OWN, UP1, k, dst1).wait_send())
        pl.when(gets3(dst3, k))(lambda: block_copy(OWN, UP3, k, dst3).wait_send())
        pl.when(gets2(below, k))(
            lambda: block_copy(UP1, UP2, k, along(-1)).wait_send())
        pl.when(gets_pairs(above, k))(lambda: product_copy(k).wait_send())
        return carry

    lax.fori_loop(0, NCH, drain, 0)


def widen_kernel(in_ref, out_ref):
    for k in range(NCH):
        for q in range(2):
            out_ref[:, q, FCH * k:FCH * k + FCH, :] = in_ref[
                k, :, FCH * q:FCH * q + FCH, :].astype(F32)


def per_device(traces):
    table = jnp.asarray(kernel_rows())
    dma = pltpu.SemaphoreType.DMA
    hbm = pl.BlockSpec(memory_space=pltpu.MemorySpace.HBM)
    stacks = pl.pallas_call(
        stack_kernel,
        out_shape=jax.ShapeDtypeStruct((NCH, CH, 2 * FCH, LAG), BF16),
        in_specs=[hbm, hbm],
        out_specs=hbm,
        scratch_shapes=[
            pltpu.VMEM((CH, WIN, NSAMP), BF16),
            pltpu.VMEM((2 * BINS, NSAMP), BF16),
            pltpu.VMEM((SEG, NCH, 2 * FCH, CH * WIN), BF16),
            pltpu.VMEM((SEG, NCH, 2 * FCH, CH * WIN), BF16),
            pltpu.VMEM((BAND, 5 * CH, DEPTH), BF16),
            pltpu.VMEM((BAND, CH, DEPTH), BF16),
            pltpu.VMEM((BAND, CH, 2 * CH), BF16),
            pltpu.VMEM((BAND, CH, 2 * CH), BF16),
            pltpu.VMEM((NCH, FCH // 2, CH, DEPTH), BF16),
            pltpu.VMEM((2, CH * FCH, 128), F32),
            pltpu.VMEM((2, LAG // 128, FCH * CH, 128), F32),
            pltpu.VMEM((2, CH, 2 * FCH, LAG), BF16),
            dma((9,)), dma((3, NCH)), dma((3, NCH)), dma, dma((4, NCH)), dma((4, NCH)),
            dma((NCH,)), dma((NCH,)), dma((NCH,)), dma((NCH,)),
            dma((NCH,)), dma((NCH,)), dma((2,)),
        ],
        compiler_params=pltpu.CompilerParams(
            collective_id=0, has_side_effects=True, vmem_limit_bytes=48 << 20),
    )(traces, table)
    part = 16
    return pl.pallas_call(
        widen_kernel,
        grid=(CH // part,),
        out_shape=jax.ShapeDtypeStruct((CH, 2, BAND, LAG), F32),
        in_specs=[pl.BlockSpec((NCH, part, 2 * FCH, LAG), lambda i: (0, i, 0, 0))],
        out_specs=pl.BlockSpec((part, 2, BAND, LAG), lambda i: (i, 0, 0, 0)),
    )(stacks)


def solution(mesh):
    return jax.shard_map(
        per_device,
        mesh=mesh,
        in_specs=(P("chain", "tm", None),),
        out_specs=P("chain", None, "tm", None),
        check_vma=False,
    )
```

```python
import math

import jax
import jax.numpy as jnp
import numpy as np
from jax import lax
from jax.experimental import pallas as pl
from jax.experimental.pallas import tpu as pltpu
from jax.sharding import PartitionSpec as P

MESH = pl.DeviceIdType.MESH
BF16 = jnp.bfloat16
F32 = jnp.float32

CH = 64
LAG = 256
BINS = 256
WIN = 32
NSAMP = 512
SEG = 4
BAND = BINS // SEG
FCH = 8
NCH = BAND // FCH
DEPTH = 2 * WIN * SEG
ROWY = 4
SCALE = 1.0 / math.sqrt(WIN * SEG)
FETCHED = ((), (2, 5), (2, 5), (3,))
FETCHED_FAR = ((), (2, 4, 6), (2, 4, 6), (2,5))
FETCHED_NEAR = (0,1,3,5,7)
AHEAD = 2
OWN_AT = (0, 2, 1)
TWO_AT = (4, 2, 1)
TWO_LAST_AT = (4, 2, 1)
PASS_AT = (2, 2, 1)
FOUR_AT = (2, 2, 1)
PAIRS_AT = (6, 2, 1)
FINISH_AT = (10, 2, 1)
FAR_LATE = 0


def tick_of(plan, k):
    offset, num, den = plan
    return offset + k * num // den


def chunk_at(plan, t, late=0):
    offset, num, den = plan
    offset = offset + late
    k = ((t - offset) * den + num - 1) // num
    fits = jnp.logical_and(t >= offset, k < NCH)
    return k, jnp.logical_and(fits, offset + k * num // den == t)


OWN, UP1, UP4, UP3, UP2 = 0, CH, 2 * CH, 3 * CH, 4 * CH


def kernel_rows():
    samples = np.arange(NSAMP, dtype=np.int32)
    freqs = np.arange(BINS, dtype=np.int32)
    phase = (samples[:, None] * freqs[None, :]) % NSAMP
    angles = np.float32(2.0 * math.pi / NSAMP) * phase.astype(np.float32)
    taper = np.float32(0.5) - np.float32(0.5) * np.cos(
        np.float32(2.0 * math.pi / NSAMP) * samples.astype(np.float32)
    )
    cosines = taper[:, None] * np.cos(angles)
    sines = -taper[:, None] * np.sin(angles)
    table = np.stack([cosines.T, sines.T], axis=0).astype(np.float32)
    table = table.reshape(2, SEG, NCH, FCH, NSAMP).transpose(1, 2, 0, 3, 4)
    return table.reshape(2 * BINS, NSAMP).astype(jnp.bfloat16)


def dot_nt(a, b):
    return lax.dot_general(a, b, (((1,), (1,)), ((), ())), preferred_element_type=F32)


def stack_kernel(tr_hbm, kt_hbm, out_ref, tr_ref, kt_ref, wt, rx, ball, lrev, osend, orecv,
                 stage, relay, prod, in_sem, a2a_send, a2a_recv, own_sem, blk_send, blk_recv,
                 hi_send, hi_recv, pass_send, stage_recv,
                 o_send, o_recv):
    chain = lax.axis_index("chain")
    me = lax.axis_index("tm")
    n_chain = lax.axis_size("chain")
    y = lax.rem(chain, ROWY)

    cols = 256
    chans = cols // WIN
    n_in = CH // chans

    def in_copy(j):
        rows = pl.ds(chans * j, chans)
        return pltpu.make_async_copy(tr_hbm.at[rows], tr_ref.at[rows], in_sem.at[j])

    def table_copy():
        return pltpu.make_async_copy(kt_hbm, kt_ref, in_sem.at[n_in])

    table_copy().start()
    for j in range(n_in):
        in_copy(j).start()

    def peer(delta):
        return lax.rem(me + delta, SEG)

    def along(delta):
        return lax.rem(chain + n_chain + delta, n_chain)

    def bits(chunks):
        return sum(1 << k for k in chunks)

    def fetched_set(i):
        place = lax.rem(i, ROWY)
        depth = lax.rem(i // ROWY, ROWY)
        mask = jnp.int32(0)
        for p in range(ROWY):
            there = place == p
            mask = jnp.where(there, bits(FETCHED[p]), mask)
            mask = jnp.where(jnp.logical_and(there, depth == ROWY - 1),
                             bits(FETCHED_FAR[p]), mask)
        return jnp.where(jnp.logical_and(place == 0, depth == 0), bits(FETCHED_NEAR), mask)

    here, below, above = chain, along(-1), along(1)
    fetched_sets = [(i, fetched_set(i)) for i in (here, below, above, 0)]

    def is_fetched(i, k):
        mask = [m for j, m in fetched_sets if j is i][0]
        return lax.rem(lax.shift_right_logical(mask, jnp.int32(k)), 2) == 1

    def paired(i, k):
        return jnp.logical_not(is_fetched(i, k))

    def gets1(i, k):
        return jnp.logical_or(i + 1 < n_chain, paired(0, k))

    def gets2(i, k):
        return jnp.logical_and(i + 2 < n_chain, is_fetched(i, k))

    def gets3(i, k):
        return jnp.logical_or(i + 3 < n_chain, jnp.logical_and(i == n_chain - 1, paired(0, k)))

    def gets4(i, k):
        extra = jnp.logical_or(i == n_chain - 4, i == n_chain - 2)
        return jnp.logical_or(i + 4 < n_chain, jnp.logical_and(extra, paired(0, k)))

    def gets_pairs(i, k):
        return jnp.logical_and(i + 2 < n_chain, paired(i, k))

    first = y == 0
    last = y == ROWY - 1
    src1 = jnp.where(last, chain - (ROWY - 1), chain + 1)
    src3 = jnp.where(first, chain + (ROWY - 1), chain - 1)
    dst1 = jnp.where(first, chain + (ROWY - 1), chain - 1)
    dst3 = jnp.where(last, chain - (ROWY - 1), chain + 1)

    barrier = pltpu.get_barrier_semaphore()

    def greet(c, t):
        pl.semaphore_signal(barrier, inc=1, device_id=(c, t), device_id_type=MESH)

    for delta in (1, 2, 3):
        greet(chain, peer(delta))
    for source in (src1, src3, along(ROWY), along(1), along(-1)):
        greet(source, me)
    greet(along(-3 * ROWY), me)
    greet(along(n_chain // 2), me)

    table_copy().wait()

    def whiten(j, carry):
        in_copy(j).wait()
        tr = tr_ref[pl.ds(chans * j, chans)].reshape(cols, NSAMP)
        spec = dot_nt(kt_ref[...], tr).reshape(SEG * NCH, 2, FCH, cols)
        re = spec[:, 0]
        im = spec[:, 1]
        mag = jnp.sqrt(re * re + im * im)
        level = jnp.sum(mag, axis=(0, 1), keepdims=True) * (1.0 / BINS)
        inv = 1.0 / (mag + 0.1 * (level + 1e-6))
        white = jnp.stack([re * inv, im * inv], axis=1)
        white = white.reshape(SEG, NCH, 2 * FCH, cols).astype(BF16)
        wt[:, :, :, pl.ds(pl.multiple_of(cols * j, cols), cols)] = white
        return carry

    lax.fori_loop(0, n_in, whiten, 0)

    pl.semaphore_wait(barrier, 10)

    def a2a_copy(delta, k):
        return pltpu.make_async_remote_copy(
            src_ref=wt.at[peer(delta), k], dst_ref=rx.at[me, k],
            send_sem=a2a_send.at[delta - 1, k], recv_sem=a2a_recv.at[delta - 1, k],
            device_id=(chain, peer(delta)), device_id_type=MESH)

    def own_copy():
        return pltpu.make_async_copy(wt.at[me], rx.at[me], own_sem)

    own_copy().start()

    def start_a2a(k, carry):
        for delta in (1, 2, 3):
            a2a_copy(delta, k).start()
        return carry

    lax.fori_loop(0, AHEAD, start_a2a, 0)
    own_copy().wait()

    def block(rows, k):
        return ball.at[pl.ds(FCH * k, FCH), pl.ds(rows, CH), :]

    def block_copy(src, dst, k, target):
        return pltpu.make_async_remote_copy(
            src_ref=block(src, k), dst_ref=block(dst, k),
            send_sem=blk_send.at[dst // CH - 1, k], recv_sem=blk_recv.at[dst // CH - 1, k],
            device_id=(target, me), device_id_type=MESH)

    HALF = FCH // 2
    depth = lax.rem(chain // ROWY, ROWY)
    upper = chain >= n_chain // 2
    far_from = jnp.logical_and(upper, depth == 0)
    passes = jnp.logical_and(upper, depth == ROWY - 1)
    far_to = depth == ROWY - 1

    def half_copy(src, dst, send, recv, target):
        return pltpu.make_async_remote_copy(
            src_ref=src, dst_ref=dst, send_sem=send, recv_sem=recv,
            device_id=target, device_id_type=MESH)

    def bins_of(rows, k, half):
        return ball.at[pl.ds(FCH * k + HALF * half, HALF), pl.ds(rows, CH), :]

    def low4(k, target):
        return half_copy(bins_of(OWN, k, 0), bins_of(UP4, k, 0),
                         blk_send.at[1, k], blk_recv.at[1, k], (target, me))

    def high4(k, target):
        return half_copy(bins_of(OWN, k, 1), bins_of(UP4, k, 1),
                         hi_send.at[k], hi_recv.at[k], (target, me))

    def stage4(k):
        return half_copy(bins_of(OWN, k, 1), stage.at[k],
                         hi_send.at[k], stage_recv.at[k], (along(3 * ROWY), me))

    def pass4(k):
        return half_copy(stage.at[k], bins_of(UP4, k, 1),
                         pass_send.at[k], hi_recv.at[k], (along(n_chain // 2), me))

    def product_copy(k):
        bins = pl.ds(FCH * k, FCH)
        return pltpu.make_async_remote_copy(
            src_ref=osend.at[bins], dst_ref=orecv.at[bins],
            send_sem=o_send.at[k], recv_sem=o_recv.at[k],
            device_id=(along(1), me), device_id_type=MESH)

    rows64 = lax.broadcasted_iota(jnp.int32, (CH, CH), 0)
    cols64 = lax.broadcasted_iota(jnp.int32, (CH, CH), 1)
    flip = (rows64 + cols64 == CH - 1).astype(F32).astype(BF16)

    def flipped(x):
        return jnp.dot(flip, x, preferred_element_type=F32).astype(BF16)

    def relayout(k):
        lane = lax.broadcasted_iota(jnp.int32, (2 * FCH, 128), 1)
        low = lane < 64
        even = lax.rem(lane // 32, 2) == 0

        def group(c4):
            at = pl.ds(pl.multiple_of(c4 * 128, 128), 128)
            x = [rx[h, k, :, at].astype(F32) for h in range(SEG)]
            a0 = jnp.where(low, x[0], pltpu.roll(x[2], 64, 1))
            a2 = jnp.where(low, pltpu.roll(x[0], 64, 1), x[2])
            a1 = jnp.where(low, x[1], pltpu.roll(x[3], 64, 1))
            a3 = jnp.where(low, pltpu.roll(x[1], 64, 1), x[3])
            o0 = jnp.where(even, a0, pltpu.roll(a1, 32, 1))
            o1 = jnp.where(even, pltpu.roll(a0, 96, 1), a1)
            o2 = jnp.where(even, a2, pltpu.roll(a3, 32, 1))
            o3 = jnp.where(even, pltpu.roll(a2, 96, 1), a3)
            for c, o in enumerate((o0, o1, o2, o3)):
                rows = pl.ds(pl.multiple_of((c4 * 4 + c) * FCH, FCH), FCH)
                relay[0, rows, :] = o[:FCH]
                relay[1, rows, :] = o[FCH:]

        def groups(i, carry):
            for u in range(4):
                group(i * 4 + u)
            return carry

        lax.fori_loop(0, CH // 16, groups, 0)
        for f in range(FCH):
            halves = [relay[p, pl.ds(f, CH, stride=FCH), :] for p in range(2)]
            x = jnp.concatenate(halves, axis=1).astype(BF16)
            ball[FCH * k + f, OWN:OWN + CH, :] = x
            lrev[FCH * k + f] = flipped(x)

    def neighbour_products(k):
        def bins(i, carry):
            for u in range(4):
                fi = FCH * k + i * 4 + u
                left = flipped(ball[fi, UP1:UP1 + CH, :])
                right = ball[fi, UP3:UP3 + CH, :]
                turned = jnp.concatenate([-right[:, 128:], right[:, :128]], axis=1)
                both = jnp.concatenate([right, turned], axis=0)
                osend[fi] = dot_nt(left, both).astype(BF16)
            return carry

        lax.fori_loop(0, FCH // 4, bins, 0)

    lane = lax.broadcasted_iota(jnp.int32, (CH, 128), 1)
    low = lane < 64
    lane3 = lax.broadcasted_iota(jnp.int32, (1, 384), 1)
    inside = (chain + lane3 // CH) < n_chain

    def products(k, fetched):
        def one_bin(f):
            fi = FCH * k + f
            x = lrev[fi]
            turned = jnp.concatenate([x[:, 128:], -x[:, :128]], axis=1)
            left = jnp.concatenate([x, turned], axis=0)
            if fetched:
                pr = dot_nt(left, ball[fi])
                pad = jnp.zeros((2 * CH, 64), F32)
                two = jnp.concatenate([pr[:, 256:], pad], axis=1)
                two = [two[:CH], two[CH:]]
            else:
                pr = dot_nt(left, ball[fi, :256, :])
                o = orecv[fi].astype(F32)
                two = [o, pltpu.roll(o, 64, 1)]
            for q in range(2):
                p0 = pr[CH * q:CH * q + CH, :128]
                p1 = pr[CH * q:CH * q + CH, 128:256]
                mid = jnp.where(low, two[q], p1)
                full = jnp.concatenate([p0, mid, p1], axis=1) * SCALE
                full = jnp.where(inside, full, 0.0)
                full = pltpu.roll(full, 384 - (CH - 1), 1, stride=1, stride_axis=0)
                for t in range(LAG // 128):
                    prod[q, t, pl.ds(f * CH, CH), :] = full[:, 128 * t:128 * t + 128]

        for f in range(FCH):
            one_bin(f)

    def to_rows(k):
        def channels(i, carry):
            for u in range(16):
                c = i * 16 + u
                for q in range(2):
                    for t in range(LAG // 128):
                        out_ref[k, c, FCH * q:FCH * q + FCH, 128 * t:128 * t + 128] = prod[
                            q, t, pl.ds(CH - 1 - c, FCH, stride=CH), :].astype(BF16)
            return carry

        lax.fori_loop(0, CH // 16, channels, 0)

    def both(a, b):
        return jnp.logical_and(a, b)

    send1_own = jnp.logical_not(first)
    send3_own = last

    late = jnp.where(far_to, FAR_LATE, 0)

    def send_two(k):
        pl.when(gets1(chain, k))(lambda: block_copy(OWN, UP1, k, dst1).wait_recv())
        pl.when(gets2(below, k))(
            lambda: block_copy(UP1, UP2, k, along(-1)).start())

    def step(t, carry):
        k_own, now = chunk_at(OWN_AT, t)

        @pl.when(now)
        def _():
            k = k_own
            for delta in (1, 2, 3):
                a2a_copy(delta, k).wait_recv()
            pl.when(k + AHEAD < NCH)(lambda: start_a2a(k + AHEAD, None))
            relayout(k)

            @pl.when(gets4(along(-ROWY), k))
            def _():
                low4(k, along(-ROWY)).start()
                pl.when(far_from)(lambda: stage4(k).start())
                pl.when(jnp.logical_not(far_from))(lambda: high4(k, along(-ROWY)).start())

            pl.when(both(send1_own, gets1(dst1, k)))(
                lambda: block_copy(OWN, UP1, k, dst1).start())
            pl.when(both(send3_own, gets3(dst3, k)))(
                lambda: block_copy(OWN, UP3, k, dst3).start())

        k_two, now = chunk_at(TWO_AT, t)

        @pl.when(both(jnp.logical_not(last), now))
        def _():
            send_two(k_two)

        k_pass, now = chunk_at(PASS_AT, t, late)

        @pl.when(both(passes, now))
        def _():
            k = k_pass

            stage4(k).wait_recv()
            pass4(k).start()

        k_four, now = chunk_at(FOUR_AT, t, late)

        @pl.when(now)
        def _():
            k = k_four

            @pl.when(gets4(chain, k))
            def _():
                low4(k, chain).wait_recv()
                high4(k, chain).wait_recv()

            pl.when(both(jnp.logical_not(send3_own), gets3(dst3, k)))(
                lambda: block_copy(UP4, UP3, k, dst3).start())
            pl.when(both(jnp.logical_not(send1_own), gets1(dst1, k)))(
                lambda: block_copy(UP4, UP1, k, dst1).start())

        k_last, now = chunk_at(TWO_LAST_AT, t, late)

        @pl.when(both(last, now))
        def _():
            send_two(k_last)

        k_pairs, now = chunk_at(PAIRS_AT, t, late)

        @pl.when(now)
        def _():
            k = k_pairs
            pl.when(gets3(chain, k))(lambda: block_copy(OWN, UP3, k, dst3).wait_recv())

            @pl.when(gets_pairs(above, k))
            def _():
                neighbour_products(k)
                product_copy(k).start()

        k_finish, now = chunk_at(FINISH_AT, t, late)

        @pl.when(now)
        def _():
            k = k_finish
            pl.when(gets2(chain, k))(lambda: block_copy(UP1, UP2, k, chain).wait_recv())
            pl.when(gets_pairs(chain, k))(lambda: product_copy(k).wait_recv())
            pl.when(is_fetched(chain, k))(lambda: products(k, True))
            pl.when(paired(chain, k))(lambda: products(k, False))
            to_rows(k)
        return carry

    lax.fori_loop(0, tick_of(FINISH_AT, NCH - 1) + 1 + FAR_LATE, step, 0)


    def drain(k, carry):
        for delta in (1, 2, 3):
            a2a_copy(delta, k).wait_send()

        @pl.when(gets4(along(-ROWY), k))
        def _():
            low4(k, along(-ROWY)).wait_send()
            high4(k, along(-ROWY)).wait_send()

        pl.when(passes)(lambda: pass4(k).wait_send())
        pl.when(gets1(dst1, k))(lambda: block_copy(OWN, UP1, k, dst1).wait_send())
        pl.when(gets3(dst3, k))(lambda: block_copy(OWN, UP3, k, dst3).wait_send())
        pl.when(gets2(below, k))(
            lambda: block_copy(UP1, UP2, k, along(-1)).wait_send())
        pl.when(gets_pairs(above, k))(lambda: product_copy(k).wait_send())
        return carry

    lax.fori_loop(0, NCH, drain, 0)


def widen_kernel(in_ref, out_ref):
    for k in range(NCH):
        for q in range(2):
            out_ref[:, q, FCH * k:FCH * k + FCH, :] = in_ref[
                k, :, FCH * q:FCH * q + FCH, :].astype(F32)


def per_device(traces):
    table = jnp.asarray(kernel_rows())
    dma = pltpu.SemaphoreType.DMA
    hbm = pl.BlockSpec(memory_space=pltpu.MemorySpace.HBM)
    stacks = pl.pallas_call(
        stack_kernel,
        out_shape=jax.ShapeDtypeStruct((NCH, CH, 2 * FCH, LAG), BF16),
        in_specs=[hbm, hbm],
        out_specs=pl.BlockSpec(memory_space=pltpu.VMEM),
        scratch_shapes=[
            pltpu.VMEM((CH, WIN, NSAMP), BF16),
            pltpu.VMEM((2 * BINS, NSAMP), BF16),
            pltpu.VMEM((SEG, NCH, 2 * FCH, CH * WIN), BF16),
            pltpu.VMEM((SEG, NCH, 2 * FCH, CH * WIN), BF16),
            pltpu.VMEM((BAND, 5 * CH, DEPTH), BF16),
            pltpu.VMEM((BAND, CH, DEPTH), BF16),
            pltpu.VMEM((BAND, CH, 2 * CH), BF16),
            pltpu.VMEM((BAND, CH, 2 * CH), BF16),
            pltpu.VMEM((NCH, FCH // 2, CH, DEPTH), BF16),
            pltpu.VMEM((2, CH * FCH, 128), F32),
            pltpu.VMEM((2, LAG // 128, FCH * CH, 128), F32),
            dma((9,)), dma((3, NCH)), dma((3, NCH)), dma, dma((4, NCH)), dma((4, NCH)),
            dma((NCH,)), dma((NCH,)), dma((NCH,)), dma((NCH,)),
            dma((NCH,)), dma((NCH,)),
        ],
        compiler_params=pltpu.CompilerParams(
            collective_id=0, has_side_effects=True, vmem_limit_bytes=58 << 20),
    )(traces, table)
    part = 16
    return pl.pallas_call(
        widen_kernel,
        grid=(CH // part,),
        out_shape=jax.ShapeDtypeStruct((CH, 2, BAND, LAG), F32),
        in_specs=[pl.BlockSpec((NCH, part, 2 * FCH, LAG), lambda i: (0, i, 0, 0))],
        out_specs=pl.BlockSpec((part, 2, BAND, LAG), lambda i: (i, 0, 0, 0)),
    )(stacks)


def solution(mesh):
    return jax.shard_map(
        per_device,
        mesh=mesh,
        in_specs=(P("chain", "tm", None),),
        out_specs=P("chain", None, "tm", None),
        check_vma=False,
    )
```

```python
import math

import jax
import jax.numpy as jnp
import numpy as np
from jax import lax
from jax.experimental import pallas as pl
from jax.experimental.pallas import tpu as pltpu
from jax.sharding import PartitionSpec as P

MESH = pl.DeviceIdType.MESH
BF16 = jnp.bfloat16
F32 = jnp.float32

CH = 64
LAG = 256
BINS = 256
WIN = 32
NSAMP = 512
SEG = 4
BAND = BINS // SEG
FCH = 8
NCH = BAND // FCH
DEPTH = 2 * WIN * SEG
ROWY = 4
SCALE = 1.0 / math.sqrt(WIN * SEG)
FETCHED = ((4,), (1, 4), (1, 4), (2,))
FETCHED_FAR = ((), (2, 4, 6), (2, 4, 6), (2,5))
FETCHED_NEAR = (0,1,3,5,7)
AHEAD = 2
OWN_AT = (0, 2, 1)
TWO_AT = (4, 2, 1)
TWO_LAST_AT = (4, 2, 1)
PASS_AT = (2, 2, 1)
FOUR_AT = (2, 2, 1)
PAIRS_AT = (6, 2, 1)
FINISH_AT = (10, 2, 1)
FAR_LATE = 0


def tick_of(plan, k):
    offset, num, den = plan
    return offset + k * num // den


def chunk_at(plan, t, late=0):
    offset, num, den = plan
    offset = offset + late
    k = ((t - offset) * den + num - 1) // num
    fits = jnp.logical_and(t >= offset, k < NCH)
    return k, jnp.logical_and(fits, offset + k * num // den == t)


OWN, UP1, UP4, UP3, UP2 = 0, CH, 2 * CH, 3 * CH, 4 * CH


def kernel_rows():
    samples = np.arange(NSAMP, dtype=np.int32)
    freqs = np.arange(BINS, dtype=np.int32)
    phase = (samples[:, None] * freqs[None, :]) % NSAMP
    angles = np.float32(2.0 * math.pi / NSAMP) * phase.astype(np.float32)
    taper = np.float32(0.5) - np.float32(0.5) * np.cos(
        np.float32(2.0 * math.pi / NSAMP) * samples.astype(np.float32)
    )
    cosines = taper[:, None] * np.cos(angles)
    sines = -taper[:, None] * np.sin(angles)
    table = np.stack([cosines.T, sines.T], axis=0).astype(np.float32)
    table = table.reshape(2, SEG, NCH, FCH, NSAMP).transpose(1, 2, 0, 3, 4)
    return table.reshape(2 * BINS, NSAMP).astype(jnp.bfloat16)


def dot_nt(a, b):
    return lax.dot_general(a, b, (((1,), (1,)), ((), ())), preferred_element_type=F32)


def stack_kernel(tr_hbm, kt_hbm, out_ref, tr_ref, kt_ref, wt, rx, ball, lrev, osend, orecv,
                 stage, relay, prod, in_sem, a2a_send, a2a_recv, own_sem, blk_send, blk_recv,
                 hi_send, hi_recv, pass_send, stage_recv,
                 o_send, o_recv):
    chain = lax.axis_index("chain")
    me = lax.axis_index("tm")
    n_chain = lax.axis_size("chain")
    y = lax.rem(chain, ROWY)

    cols = 256
    chans = cols // WIN
    n_in = CH // chans

    def in_copy(j):
        rows = pl.ds(chans * j, chans)
        return pltpu.make_async_copy(tr_hbm.at[rows], tr_ref.at[rows], in_sem.at[j])

    def table_copy():
        return pltpu.make_async_copy(kt_hbm, kt_ref, in_sem.at[n_in])

    table_copy().start()
    for j in range(n_in):
        in_copy(j).start()

    def peer(delta):
        return lax.rem(me + delta, SEG)

    def along(delta):
        return lax.rem(chain + n_chain + delta, n_chain)

    def bits(chunks):
        return sum(1 << k for k in chunks)

    def fetched_set(i):
        place = lax.rem(i, ROWY)
        depth = lax.rem(i // ROWY, ROWY)
        mask = jnp.int32(0)
        for p in range(ROWY):
            there = place == p
            mask = jnp.where(there, bits(FETCHED[p]), mask)
            mask = jnp.where(jnp.logical_and(there, depth == ROWY - 1),
                             bits(FETCHED_FAR[p]), mask)
        return jnp.where(jnp.logical_and(place == 0, depth == 0), bits(FETCHED_NEAR), mask)

    here, below, above = chain, along(-1), along(1)
    fetched_sets = [(i, fetched_set(i)) for i in (here, below, above, 0)]

    def is_fetched(i, k):
        mask = [m for j, m in fetched_sets if j is i][0]
        return lax.rem(lax.shift_right_logical(mask, jnp.int32(k)), 2) == 1

    def paired(i, k):
        return jnp.logical_not(is_fetched(i, k))

    def gets1(i, k):
        return jnp.logical_or(i + 1 < n_chain, paired(0, k))

    def gets2(i, k):
        return jnp.logical_and(i + 2 < n_chain, is_fetched(i, k))

    def gets3(i, k):
        return jnp.logical_or(i + 3 < n_chain, jnp.logical_and(i == n_chain - 1, paired(0, k)))

    def gets4(i, k):
        extra = jnp.logical_or(i == n_chain - 4, i == n_chain - 2)
        return jnp.logical_or(i + 4 < n_chain, jnp.logical_and(extra, paired(0, k)))

    def gets_pairs(i, k):
        return jnp.logical_and(i + 2 < n_chain, paired(i, k))

    first = y == 0
    last = y == ROWY - 1
    src1 = jnp.where(last, chain - (ROWY - 1), chain + 1)
    src3 = jnp.where(first, chain + (ROWY - 1), chain - 1)
    dst1 = jnp.where(first, chain + (ROWY - 1), chain - 1)
    dst3 = jnp.where(last, chain - (ROWY - 1), chain + 1)

    barrier = pltpu.get_barrier_semaphore()

    def greet(c, t):
        pl.semaphore_signal(barrier, inc=1, device_id=(c, t), device_id_type=MESH)

    for delta in (1, 2, 3):
        greet(chain, peer(delta))
    for source in (src1, src3, along(ROWY), along(1), along(-1)):
        greet(source, me)
    greet(along(-3 * ROWY), me)
    greet(along(n_chain // 2), me)

    table_copy().wait()

    def whiten(j, carry):
        in_copy(j).wait()
        tr = tr_ref[pl.ds(chans * j, chans)].reshape(cols, NSAMP)
        spec = dot_nt(kt_ref[...], tr).reshape(SEG * NCH, 2, FCH, cols)
        re = spec[:, 0]
        im = spec[:, 1]
        mag = jnp.sqrt(re * re + im * im)
        level = jnp.sum(mag, axis=(0, 1), keepdims=True) * (1.0 / BINS)
        inv = 1.0 / (mag + 0.1 * (level + 1e-6))
        white = jnp.stack([re * inv, im * inv], axis=1)
        white = white.reshape(SEG, NCH, 2 * FCH, cols).astype(BF16)
        wt[:, :, :, pl.ds(pl.multiple_of(cols * j, cols), cols)] = white
        return carry

    lax.fori_loop(0, n_in, whiten, 0)

    pl.semaphore_wait(barrier, 10)

    def a2a_copy(delta, k):
        return pltpu.make_async_remote_copy(
            src_ref=wt.at[peer(delta), k], dst_ref=rx.at[me, k],
            send_sem=a2a_send.at[delta - 1, k], recv_sem=a2a_recv.at[delta - 1, k],
            device_id=(chain, peer(delta)), device_id_type=MESH)

    def own_copy():
        return pltpu.make_async_copy(wt.at[me], rx.at[me], own_sem)

    own_copy().start()

    def start_a2a(k, carry):
        for delta in (1, 2, 3):
            a2a_copy(delta, k).start()
        return carry

    lax.fori_loop(0, AHEAD, start_a2a, 0)
    own_copy().wait()

    def block(rows, k):
        return ball.at[pl.ds(FCH * k, FCH), pl.ds(rows, CH), :]

    def block_copy(src, dst, k, target):
        return pltpu.make_async_remote_copy(
            src_ref=block(src, k), dst_ref=block(dst, k),
            send_sem=blk_send.at[dst // CH - 1, k], recv_sem=blk_recv.at[dst // CH - 1, k],
            device_id=(target, me), device_id_type=MESH)

    HALF = FCH // 2
    depth = lax.rem(chain // ROWY, ROWY)
    upper = chain >= n_chain // 2
    far_from = jnp.logical_and(upper, depth == 0)
    passes = jnp.logical_and(upper, depth == ROWY - 1)
    far_to = depth == ROWY - 1

    def half_copy(src, dst, send, recv, target):
        return pltpu.make_async_remote_copy(
            src_ref=src, dst_ref=dst, send_sem=send, recv_sem=recv,
            device_id=target, device_id_type=MESH)

    def bins_of(rows, k, half):
        return ball.at[pl.ds(FCH * k + HALF * half, HALF), pl.ds(rows, CH), :]

    def low4(k, target):
        return half_copy(bins_of(OWN, k, 0), bins_of(UP4, k, 0),
                         blk_send.at[1, k], blk_recv.at[1, k], (target, me))

    def high4(k, target):
        return half_copy(bins_of(OWN, k, 1), bins_of(UP4, k, 1),
                         hi_send.at[k], hi_recv.at[k], (target, me))

    def stage4(k):
        return half_copy(bins_of(OWN, k, 1), stage.at[k],
                         hi_send.at[k], stage_recv.at[k], (along(3 * ROWY), me))

    def pass4(k):
        return half_copy(stage.at[k], bins_of(UP4, k, 1),
                         pass_send.at[k], hi_recv.at[k], (along(n_chain // 2), me))

    def product_copy(k):
        bins = pl.ds(FCH * k, FCH)
        return pltpu.make_async_remote_copy(
            src_ref=osend.at[bins], dst_ref=orecv.at[bins],
            send_sem=o_send.at[k], recv_sem=o_recv.at[k],
            device_id=(along(1), me), device_id_type=MESH)

    rows64 = lax.broadcasted_iota(jnp.int32, (CH, CH), 0)
    cols64 = lax.broadcasted_iota(jnp.int32, (CH, CH), 1)
    flip = (rows64 + cols64 == CH - 1).astype(F32).astype(BF16)

    def flipped(x):
        return jnp.dot(flip, x, preferred_element_type=F32).astype(BF16)

    def relayout(k):
        lane = lax.broadcasted_iota(jnp.int32, (2 * FCH, 128), 1)
        low = lane < 64
        even = lax.rem(lane // 32, 2) == 0

        def group(c4):
            at = pl.ds(pl.multiple_of(c4 * 128, 128), 128)
            x = [rx[h, k, :, at].astype(F32) for h in range(SEG)]
            a0 = jnp.where(low, x[0], pltpu.roll(x[2], 64, 1))
            a2 = jnp.where(low, pltpu.roll(x[0], 64, 1), x[2])
            a1 = jnp.where(low, x[1], pltpu.roll(x[3], 64, 1))
            a3 = jnp.where(low, pltpu.roll(x[1], 64, 1), x[3])
            o0 = jnp.where(even, a0, pltpu.roll(a1, 32, 1))
            o1 = jnp.where(even, pltpu.roll(a0, 96, 1), a1)
            o2 = jnp.where(even, a2, pltpu.roll(a3, 32, 1))
            o3 = jnp.where(even, pltpu.roll(a2, 96, 1), a3)
            for c, o in enumerate((o0, o1, o2, o3)):
                rows = pl.ds(pl.multiple_of((c4 * 4 + c) * FCH, FCH), FCH)
                relay[0, rows, :] = o[:FCH]
                relay[1, rows, :] = o[FCH:]

        def groups(i, carry):
            for u in range(4):
                group(i * 4 + u)
            return carry

        lax.fori_loop(0, CH // 16, groups, 0)
        for f in range(FCH):
            halves = [relay[p, pl.ds(f, CH, stride=FCH), :] for p in range(2)]
            x = jnp.concatenate(halves, axis=1).astype(BF16)
            ball[FCH * k + f, OWN:OWN + CH, :] = x
            lrev[FCH * k + f] = flipped(x)

    def neighbour_products(k):
        def bins(i, carry):
            for u in range(4):
                fi = FCH * k + i * 4 + u
                left = flipped(ball[fi, UP1:UP1 + CH, :])
                right = ball[fi, UP3:UP3 + CH, :]
                turned = jnp.concatenate([-right[:, 128:], right[:, :128]], axis=1)
                both = jnp.concatenate([right, turned], axis=0)
                osend[fi] = dot_nt(left, both).astype(BF16)
            return carry

        lax.fori_loop(0, FCH // 4, bins, 0)

    lane = lax.broadcasted_iota(jnp.int32, (CH, 128), 1)
    low = lane < 64
    lane3 = lax.broadcasted_iota(jnp.int32, (1, 384), 1)
    inside = (chain + lane3 // CH) < n_chain

    def products(k, fetched):
        def one_bin(f):
            fi = FCH * k + f
            x = lrev[fi]
            turned = jnp.concatenate([x[:, 128:], -x[:, :128]], axis=1)
            left = jnp.concatenate([x, turned], axis=0)
            if fetched:
                pr = dot_nt(left, ball[fi])
                pad = jnp.zeros((2 * CH, 64), F32)
                two = jnp.concatenate([pr[:, 256:], pad], axis=1)
                two = [two[:CH], two[CH:]]
            else:
                pr = dot_nt(left, ball[fi, :256, :])
                o = orecv[fi].astype(F32)
                two = [o, pltpu.roll(o, 64, 1)]
            for q in range(2):
                p0 = pr[CH * q:CH * q + CH, :128]
                p1 = pr[CH * q:CH * q + CH, 128:256]
                mid = jnp.where(low, two[q], p1)
                full = jnp.concatenate([p0, mid, p1], axis=1) * SCALE
                full = jnp.where(inside, full, 0.0)
                full = pltpu.roll(full, 384 - (CH - 1), 1, stride=1, stride_axis=0)
                for t in range(LAG // 128):
                    prod[q, t, pl.ds(f * CH, CH), :] = full[:, 128 * t:128 * t + 128]

        for f in range(FCH):
            one_bin(f)

    def to_rows(k):
        def channels(i, carry):
            for u in range(16):
                c = i * 16 + u
                for q in range(2):
                    for t in range(LAG // 128):
                        out_ref[k, c, FCH * q:FCH * q + FCH, 128 * t:128 * t + 128] = prod[
                            q, t, pl.ds(CH - 1 - c, FCH, stride=CH), :].astype(BF16)
            return carry

        lax.fori_loop(0, CH // 16, channels, 0)

    def both(a, b):
        return jnp.logical_and(a, b)

    send1_own = jnp.logical_not(first)
    send3_own = last

    late = jnp.where(far_to, FAR_LATE, 0)

    def send_two(k):
        pl.when(gets1(chain, k))(lambda: block_copy(OWN, UP1, k, dst1).wait_recv())
        pl.when(gets2(below, k))(
            lambda: block_copy(UP1, UP2, k, along(-1)).start())

    def step(t, carry):
        k_own, now = chunk_at(OWN_AT, t)

        @pl.when(now)
        def _():
            k = k_own
            for delta in (1, 2, 3):
                a2a_copy(delta, k).wait_recv()
            pl.when(k + AHEAD < NCH)(lambda: start_a2a(k + AHEAD, None))
            relayout(k)

            @pl.when(gets4(along(-ROWY), k))
            def _():
                low4(k, along(-ROWY)).start()
                pl.when(far_from)(lambda: stage4(k).start())
                pl.when(jnp.logical_not(far_from))(lambda: high4(k, along(-ROWY)).start())

            pl.when(both(send1_own, gets1(dst1, k)))(
                lambda: block_copy(OWN, UP1, k, dst1).start())
            pl.when(both(send3_own, gets3(dst3, k)))(
                lambda: block_copy(OWN, UP3, k, dst3).start())

        k_two, now = chunk_at(TWO_AT, t)

        @pl.when(both(jnp.logical_not(last), now))
        def _():
            send_two(k_two)

        k_pass, now = chunk_at(PASS_AT, t, late)

        @pl.when(both(passes, now))
        def _():
            k = k_pass

            stage4(k).wait_recv()
            pass4(k).start()

        k_four, now = chunk_at(FOUR_AT, t, late)

        @pl.when(now)
        def _():
            k = k_four

            @pl.when(gets4(chain, k))
            def _():
                low4(k, chain).wait_recv()
                high4(k, chain).wait_recv()

            pl.when(both(jnp.logical_not(send3_own), gets3(dst3, k)))(
                lambda: block_copy(UP4, UP3, k, dst3).start())
            pl.when(both(jnp.logical_not(send1_own), gets1(dst1, k)))(
                lambda: block_copy(UP4, UP1, k, dst1).start())

        k_last, now = chunk_at(TWO_LAST_AT, t, late)

        @pl.when(both(last, now))
        def _():
            send_two(k_last)

        k_pairs, now = chunk_at(PAIRS_AT, t, late)

        @pl.when(now)
        def _():
            k = k_pairs
            pl.when(gets3(chain, k))(lambda: block_copy(OWN, UP3, k, dst3).wait_recv())

            @pl.when(gets_pairs(above, k))
            def _():
                neighbour_products(k)
                product_copy(k).start()

        k_finish, now = chunk_at(FINISH_AT, t, late)

        @pl.when(now)
        def _():
            k = k_finish
            pl.when(gets2(chain, k))(lambda: block_copy(UP1, UP2, k, chain).wait_recv())
            pl.when(gets_pairs(chain, k))(lambda: product_copy(k).wait_recv())
            pl.when(is_fetched(chain, k))(lambda: products(k, True))
            pl.when(paired(chain, k))(lambda: products(k, False))
            to_rows(k)
        return carry

    lax.fori_loop(0, tick_of(FINISH_AT, NCH - 1) + 1 + FAR_LATE, step, 0)


    def drain(k, carry):
        for delta in (1, 2, 3):
            a2a_copy(delta, k).wait_send()

        @pl.when(gets4(along(-ROWY), k))
        def _():
            low4(k, along(-ROWY)).wait_send()
            high4(k, along(-ROWY)).wait_send()

        pl.when(passes)(lambda: pass4(k).wait_send())
        pl.when(gets1(dst1, k))(lambda: block_copy(OWN, UP1, k, dst1).wait_send())
        pl.when(gets3(dst3, k))(lambda: block_copy(OWN, UP3, k, dst3).wait_send())
        pl.when(gets2(below, k))(
            lambda: block_copy(UP1, UP2, k, along(-1)).wait_send())
        pl.when(gets_pairs(above, k))(lambda: product_copy(k).wait_send())
        return carry

    lax.fori_loop(0, NCH, drain, 0)


def widen_kernel(in_ref, out_ref):
    for k in range(NCH):
        for q in range(2):
            out_ref[:, q, FCH * k:FCH * k + FCH, :] = in_ref[
                k, :, FCH * q:FCH * q + FCH, :].astype(F32)


def per_device(traces):
    table = jnp.asarray(kernel_rows())
    dma = pltpu.SemaphoreType.DMA
    hbm = pl.BlockSpec(memory_space=pltpu.MemorySpace.HBM)
    stacks = pl.pallas_call(
        stack_kernel,
        out_shape=jax.ShapeDtypeStruct((NCH, CH, 2 * FCH, LAG), BF16),
        in_specs=[hbm, hbm],
        out_specs=pl.BlockSpec(memory_space=pltpu.VMEM),
        scratch_shapes=[
            pltpu.VMEM((CH, WIN, NSAMP), BF16),
            pltpu.VMEM((2 * BINS, NSAMP), BF16),
            pltpu.VMEM((SEG, NCH, 2 * FCH, CH * WIN), BF16),
            pltpu.VMEM((SEG, NCH, 2 * FCH, CH * WIN), BF16),
            pltpu.VMEM((BAND, 5 * CH, DEPTH), BF16),
            pltpu.VMEM((BAND, CH, DEPTH), BF16),
            pltpu.VMEM((BAND, CH, 2 * CH), BF16),
            pltpu.VMEM((BAND, CH, 2 * CH), BF16),
            pltpu.VMEM((NCH, FCH // 2, CH, DEPTH), BF16),
            pltpu.VMEM((2, CH * FCH, 128), F32),
            pltpu.VMEM((2, LAG // 128, FCH * CH, 128), F32),
            dma((9,)), dma((3, NCH)), dma((3, NCH)), dma, dma((4, NCH)), dma((4, NCH)),
            dma((NCH,)), dma((NCH,)), dma((NCH,)), dma((NCH,)),
            dma((NCH,)), dma((NCH,)),
        ],
        compiler_params=pltpu.CompilerParams(
            collective_id=0, has_side_effects=True, vmem_limit_bytes=58 << 20),
    )(traces, table)
    part = 16
    return pl.pallas_call(
        widen_kernel,
        grid=(CH // part,),
        out_shape=jax.ShapeDtypeStruct((CH, 2, BAND, LAG), F32),
        in_specs=[pl.BlockSpec((NCH, part, 2 * FCH, LAG), lambda i: (0, i, 0, 0))],
        out_specs=pl.BlockSpec((part, 2, BAND, LAG), lambda i: (i, 0, 0, 0)),
    )(stacks)


def solution(mesh):
    return jax.shard_map(
        per_device,
        mesh=mesh,
        in_specs=(P("chain", "tm", None),),
        out_specs=P("chain", None, "tm", None),
        check_vma=False,
    )
```
